1024 devices in a mesh: fifth: 16 (over y, z_hi), space: 64 (over z_lo, x, core).
Axes of the slice: x: 4, y: 4, z: 32 (z_hi: 4, z_lo: 8; z = z_hi * 8 + z_lo), core: 2. Of those that a mesh axis runs over, the one named last changes fastest.
Arguments:
- spinor: float32 [32, 24, 64, 512], P('fifth', None, 'space'), may hold values from -6 to 6
- gauge_links: float32 [4, 18, 64, 512], P(None, None, 'space'), may hold values from -1 to 1, as said below
Outputs:
- filtered: float32 [32, 24, 64, 512], P('fifth', None, 'space')
The draws below stay inside these ranges and needn't reach their ends.
Inputs may be any that keep to these rules, and one draw needn't show every extreme that they name: `gauge_links`: every link is a special unitary 3 x 3 complex matrix.
All inputs are finite; a program needn't handle non-finite values.
Results may differ from the reference program's by a relative error of at most 0.00002.
Values sent between devices are 32-bit elements; how exact they have to be, the bound alone decides.
A program may use at most 32 MiB of HBM per device.

```python
import jax
import jax.numpy as jnp
import numpy as np

L = 8
DEGREE = 4
SITES = 512
NT = 64
L5 = 32


def normalise(vectors):
    length = jnp.sqrt(jnp.sum(vectors * vectors, axis=(1, 2), keepdims=True))
    return vectors / length


def draw_gauge_links(key, part):
    first_key = jax.random.fold_in(key, 11)
    second_key = jax.random.fold_in(key, 23)
    shape = (4, 3, 2, NT, SITES)
    first = jnp.clip(0.6 * jax.random.normal(first_key, shape, jnp.float32), -1.0, 1.0)
    second = jnp.clip(0.6 * jax.random.normal(second_key, shape, jnp.float32), -1.0, 1.0)
    first_offset = np.zeros((1, 3, 2, 1, 1), np.float32)
    first_offset[0, 0, 0, 0, 0] = 3.0
    second_offset = np.zeros((1, 3, 2, 1, 1), np.float32)
    second_offset[0, 1, 0, 0, 0] = 3.0
    first = first + jnp.asarray(first_offset)
    second = second + jnp.asarray(second_offset)
    unit_one = normalise(first)
    one_re = unit_one[:, :, 0]
    one_im = unit_one[:, :, 1]
    second_re = second[:, :, 0]
    second_im = second[:, :, 1]
    inner_re = jnp.sum(one_re * second_re + one_im * second_im, axis=1, keepdims=True)
    inner_im = jnp.sum(one_re * second_im - one_im * second_re, axis=1, keepdims=True)
    rest_re = second_re - (inner_re * one_re - inner_im * one_im)
    rest_im = second_im - (inner_re * one_im + inner_im * one_re)
    unit_two = normalise(jnp.stack([rest_re, rest_im], axis=2))
    two_re = unit_two[:, :, 0]
    two_im = unit_two[:, :, 1]
    third_rows = []
    for index in range(3):
        left = (index + 1) % 3
        right = (index + 2) % 3
        cross_re = one_re[:, left] * two_re[:, right] - one_im[:, left] * two_im[:, right] - (one_re[:, right] * two_re[:, left] - one_im[:, right] * two_im[:, left])
        cross_im = one_re[:, left] * two_im[:, right] + one_im[:, left] * two_re[:, right] - (one_re[:, right] * two_im[:, left] + one_im[:, right] * two_re[:, left])
        third_rows.append(jnp.stack([cross_re, -cross_im], axis=1))
    unit_three = jnp.stack(third_rows, axis=1)
    matrix = jnp.stack([unit_one, unit_two, unit_three], axis=1)
    return matrix.reshape(4, 18, NT, SITES).astype(jnp.float32)


def shard_levels(stream_key, shape, cuts, least, top_value):
    def one(dim, blocks):
        steps = jax.random.uniform(jax.random.fold_in(jax.random.fold_in(stream_key, 6), dim), (blocks,), jnp.float32, least / len(cuts), top_value / len(cuts))
        return jnp.repeat(jnp.exp(steps), shape[dim] // blocks).reshape((-1,) + (1,) * (len(shape) - dim - 1))

    loudness = one(*cuts[0])
    for cut in cuts[1:]:
        loudness = loudness * one(*cut)
    return loudness


def bell_draw(rng, shape, scale, bound, shards=(), kind=jnp.bfloat16):
    loudness = shard_levels(rng, shape, shards, -0.22, 0.18) if shards else 1.0
    drawn = jax.random.normal(rng, shape, jnp.float32) * scale * loudness
    return jnp.minimum(jnp.maximum(drawn, -bound), bound).astype(kind)


def setup_inputs(seed: int = 0) -> dict:
    key_list = jax.random.split(jax.random.key(seed), 3)
    spinor = bell_draw(key_list[0], (L5, 24, NT, SITES), 1.0, 6.0, ((0, 16), (2, 64)), jnp.float32)
    gauge_links = draw_gauge_links(jax.random.fold_in(key_list[2], 71), 0)
    return {"spinor": spinor, "gauge_links": gauge_links}


wall_height = 1.8
quark_mass = 0.1
filter_center = 0.5
filter_radius = 8.0

gamma_block = (((1, 1), (0, 1)), ((1, 2), (0, 0)), ((0, 1), (1, 3)), ((0, 0), (1, 0)))
gamma_adjoint = (((1, 3), (0, 3)), ((1, 0), (0, 2)), ((0, 3), (1, 1)), ((0, 0), (1, 0)))


def times_unit(values, quarter):
    for repeat in range(quarter % 4):
        values = jnp.stack([-values[..., 1, :, :], values[..., 0, :, :]], axis=-3)
    return values


def project(current, direction, parity):
    halves_list = []
    for top_row in range(2):
        source, quarter = gamma_block[direction][top_row]
        blended = times_unit(current[..., 2 + source, :, :, :, :], quarter)
        halves_list.append(current[..., top_row, :, :, :, :] + parity * blended)
    return jnp.stack(halves_list, axis=-5)


def rebuild(half_spinor, direction, parity):
    lower_part = []
    for row_index in range(2):
        source, quarter = gamma_adjoint[direction][row_index]
        lower_part.append(parity * times_unit(half_spinor[..., source, :, :, :, :], quarter))
    return jnp.concatenate([half_spinor, jnp.stack(lower_part, axis=-5)], axis=-5)


def colour_mul(link_matrix, half_spinor, dagger):
    link_re = link_matrix[:, :, 0]
    link_im = link_matrix[:, :, 1]
    if dagger:
        link_re = jnp.swapaxes(link_re, 0, 1)
        link_im = -jnp.swapaxes(link_im, 0, 1)
    result_re = None
    result_im = None
    for column in range(3):
        half_re = half_spinor[..., column:column + 1, 0, :, :]
        half_im = half_spinor[..., column:column + 1, 1, :, :]
        term_re = link_re[:, column] * half_re - link_im[:, column] * half_im
        term_im = link_re[:, column] * half_im + link_im[:, column] * half_re
        if result_re is None:
            result_re, result_im = term_re, term_im
        else:
            result_re = result_re + term_re
            result_im = result_im + term_im
    return jnp.stack([result_re, result_im], axis=-3)


def space_shift(values, stride, extent, forward):
    position = (jnp.arange(values.shape[-1]) // stride) % extent
    if forward:
        inside_roll = jnp.roll(values, -stride, axis=-1)
        outside_roll = jnp.roll(values, (extent - 1) * stride, axis=-1)
        return jnp.where(position == extent - 1, outside_roll, inside_roll)
    inside_roll = jnp.roll(values, stride, axis=-1)
    outside_roll = jnp.roll(values, -(extent - 1) * stride, axis=-1)
    return jnp.where(position == 0, outside_roll, inside_roll)


def space_hops(current, gauge, extent):
    summed = jnp.zeros_like(current)
    for direction in range(3):
        stride = extent ** direction
        forward_half = space_shift(project(current, direction, -1.0), stride, extent, True)
        summed = summed + rebuild(colour_mul(gauge[direction], forward_half, False), direction, -1.0)
        behind = colour_mul(gauge[direction], project(current, direction, 1.0), True)
        summed = summed + rebuild(space_shift(behind, stride, extent, False), direction, 1.0)
    return summed


def chiral_sign(current):
    return jnp.concatenate([current[:, 0:2], -current[:, 2:4]], axis=1)


def fifth_term(current):
    count = current.shape[0]
    slice_index = jnp.arange(count).reshape(-1, 1, 1, 1, 1, 1)
    down_half = jnp.roll(current[:, 0:2], 1, axis=0) * jnp.where(slice_index == 0, -quark_mass, 1.0)
    up_half = jnp.roll(current[:, 2:4], -1, axis=0) * jnp.where(slice_index == count - 1, -quark_mass, 1.0)
    return jnp.concatenate([down_half, up_half], axis=1)


def dirac(current, gauge):
    hop_sum = space_hops(current, gauge, L)
    count = current.shape[-2]
    time_index = jnp.arange(count).reshape(-1, 1)
    forward_half = jnp.roll(project(current, 3, -1.0), -1, axis=-2) * jnp.where(time_index == count - 1, -1.0, 1.0)
    hop_sum = hop_sum + rebuild(colour_mul(gauge[3], forward_half, False), 3, -1.0)
    behind = jnp.roll(colour_mul(gauge[3], project(current, 3, 1.0), True), 1, axis=-2) * jnp.where(time_index == 0, -1.0, 1.0)
    hop_sum = hop_sum + rebuild(behind, 3, 1.0)
    return (5.0 - wall_height) * current - 0.5 * hop_sum - fifth_term(current)


def apply_hermitian(current, gauge):
    return jnp.flip(chiral_sign(dirac(current, gauge)), axis=0)


def reference(spinor, gauge_links):
    current = spinor.reshape(L5, 4, 3, 2, NT, SITES)
    gauge = gauge_links.reshape(4, 3, 3, 2, NT, SITES)
    previous = current
    current = (apply_hermitian(previous, gauge) - filter_center * previous) / filter_radius
    for order in range(1, DEGREE):
        following = 2.0 * (apply_hermitian(current, gauge) - filter_center * current) / filter_radius - previous
        previous, current = current, following
    return current.reshape(L5, 24, NT, SITES)
```

```python
import functools

import jax
import jax.numpy as jnp
from jax import lax
from jax.experimental import pallas as pl
from jax.experimental.pallas import tpu as pltpu
from jax.sharding import PartitionSpec as P

MESH = pl.DeviceIdType.MESH
wall_height = 1.8
quark_mass = 0.1
filter_center = 0.5
filter_radius = 8.0
DEGREE = 4
gamma_block = (((1, 1), (0, 1)), ((1, 2), (0, 0)), ((0, 1), (1, 3)), ((0, 0), (1, 0)))
gamma_adjoint = (((1, 3), (0, 3)), ((1, 0), (0, 2)), ((0, 3), (1, 1)), ((0, 0), (1, 0)))
NX, NY, NHI, NC = 4, 4, 4, 2
TP, TM, KP, KM, SP, SM = range(6)


def unit_part(quarter, part):
    if part == 0:
        return ((1.0, 0), (-1.0, 1), (-1.0, 0), (1.0, 1))[quarter]
    return ((1.0, 1), (1.0, 0), (-1.0, 1), (-1.0, 0))[quarter]


def plus(value, sign, term):
    return value + term if sign > 0 else value - term


def comp(spin, colour, part):
    return (spin * 3 + colour) * 2 + part


def project(field, direction, parity):
    half = []
    for row in range(2):
        source, quarter = gamma_block[direction][row]
        for colour in range(3):
            for part in range(2):
                sign, other = unit_part(quarter, part)
                half.append(
                    plus(field(comp(row, colour, part)), parity * sign, field(comp(2 + source, colour, other)))
                )
    return half


def add_rebuilt(total, half, direction, parity):
    for row in range(2):
        source, quarter = gamma_adjoint[direction][row]
        for colour in range(3):
            for part in range(2):
                n = comp(row, colour, part)
                total[n] = total[n] + half[n]
                sign, other = unit_part(quarter, part)
                m = comp(2 + row, colour, part)
                total[m] = plus(total[m], parity * sign, half[comp(source, colour, other)])


def colour_mul(link, half, dagger):
    result = [None] * 12
    for row in range(3):
        for column in range(3):
            if dagger:
                u_re, u_im, sign = link(column, row, 0), link(column, row, 1), -1.0
            else:
                u_re, u_im, sign = link(row, column, 0), link(row, column, 1), 1.0
            for spin in range(2):
                h_re, h_im = half[comp(spin, column, 0)], half[comp(spin, column, 1)]
                re = plus(u_re * h_re, -sign, u_im * h_im)
                im = plus(u_re * h_im, sign, u_im * h_re)
                r, i = comp(spin, row, 0), comp(spin, row, 1)
                result[r] = re if column == 0 else result[r] + re
                result[i] = im if column == 0 else result[i] + im
    return result


def kernel(
    nlo,
    sp_ref,
    g_ref,
    out_ref,
    stage,
    gstage,
    psi_in,
    g_in,
    links,
    field,
    tsend,
    trecv,
    ksend,
    krecv,
    klocal,
    ssend,
    srecv,
    ostage,
    o_in,
    send1,
    recv1,
    sendg,
    recvg,
    sendh,
    recvh,
    send2,
    recv2,
    local,
):
    nz = NHI * nlo
    nt = nz * NC
    f = lax.axis_index("fifth")
    p = lax.axis_index("space")
    y, zhi = lax.div(f, NHI), lax.rem(f, NHI)
    zlo, x, c = lax.div(p, NX * NC), lax.rem(lax.div(p, NC), NX), lax.rem(p, NC)
    z = zhi * nlo + zlo

    def device(dx, dy, dz, dc):
        return (dy * NHI + lax.div(dz, nlo), lax.rem(dz, nlo) * (NX * NC) + dx * NC + dc)

    z_to = lax.div(p, NC)
    upper = f >= 8
    folded = jnp.where(upper, 15 - f, f)
    y_to = lax.div(folded, 2)
    slot = jnp.where(upper, 2, 0) + lax.rem(folded, 2)
    flip = jnp.where(upper, 1, 0)
    ahead = lax.rem(z_to - zlo + nz, nz)
    gives_links = zhi == lax.rem(lax.div(ahead + nlo // 2, nlo), NHI)
    to_self = (y_to == y) & (z_to == z)
    t = z * NC + c
    sources = (2 * y, 2 * y + 1, 15 - 2 * y, 14 - 2 * y)
    ahead_me = lax.rem(z - lax.div(t, NX * NC) + nz, nz)
    link_hi = lax.rem(lax.div(ahead_me + nlo // 2, nlo), NHI)

    t_up, t_down = lax.rem(t + 1, nt), lax.rem(t + nt - 1, nt)
    near = {
        TP: device(x, y, lax.div(t_up, NC), lax.rem(t_up, NC)),
        TM: device(x, y, lax.div(t_down, NC), lax.rem(t_down, NC)),
        KP: device(lax.rem(x + 1, NX), y, z, c),
        KM: device(lax.rem(x + NX - 1, NX), y, z, c),
        SP: device(x, jnp.minimum(y + 1, NY - 1), z, c),
        SM: device(x, jnp.maximum(y - 1, 0), z, c),
    }

    barrier = pltpu.get_barrier_semaphore()

    def greet(device_id):
        pl.semaphore_signal(barrier, inc=1, device_id=device_id, device_id_type=MESH)

    for q in range(NX):

        @pl.when(jnp.logical_not(to_self & (x == q)))
        def _():
            greet(device(q, y_to, z_to, c))

    for n in range(4):

        @pl.when(jnp.logical_not(to_self & (slot == n)))
        def _():
            greet((sources[n], t))

    for side in (TP, TM, KP, KM):
        greet(near[side])

    @pl.when(y < NY - 1)
    def _():
        greet(near[SP])

    @pl.when(y > 0)
    def _():
        greet(near[SM])

    for q in range(NX):
        for s in range(2):
            for b in range(3):
                row = pl.multiple_of(q * 48 + lax.rem(s + flip, 2) * 24 + b * 8, 8)
                stage[pl.ds(row, 8), :] = sp_ref[pl.ds((s * 24 + b * 8) * 4 + q, 8, stride=4), :]
        for mu in range(4):
            first = g_ref[pl.ds(mu * 72 + q, 8, stride=4), :]
            gstage[q * 48 + mu * 12 : q * 48 + mu * 12 + 8, :] = first
            last = g_ref[pl.ds(mu * 72 + 32 + q, 4, stride=4), :]
            gstage[q * 48 + mu * 12 + 8 : q * 48 + mu * 12 + 12, :] = last

    count = 12 - jnp.where(to_self, 2, 0) + jnp.where(y > 0, 1, 0) + jnp.where(y < NY - 1, 1, 0)
    pl.semaphore_wait(barrier, count)

    def block(ref, n):
        start = n * 48
        return ref.at[pl.ds(start if isinstance(n, int) else pl.multiple_of(start, 8), 48), :]

    def out_copy(q):
        return pltpu.make_async_remote_copy(
            src_ref=block(stage, q),
            dst_ref=block(psi_in, slot),
            send_sem=send1.at[q],
            recv_sem=recv1.at[slot],
            device_id=device(q, y_to, z_to, c),
            device_id_type=MESH,
        )

    def link_copy(q):
        return pltpu.make_async_remote_copy(
            src_ref=block(gstage, q),
            dst_ref=g_in,
            send_sem=sendg.at[q],
            recv_sem=recvg.at[0],
            device_id=device(q, y_to, z_to, c),
            device_id_type=MESH,
        )

    for q in range(NX):
        other = jnp.logical_not(to_self & (x == q))

        @pl.when(other)
        def _():
            out_copy(q).start()

        @pl.when(other & gives_links)
        def _():
            link_copy(q).start()

    @pl.when(to_self)
    def _():
        mine = pltpu.make_async_copy(block(stage, x), block(psi_in, slot), local.at[0])
        mine.start()
        mine.wait()

    @pl.when(to_self & gives_links)
    def _():
        mine = pltpu.make_async_copy(block(gstage, x), g_in, local.at[1])
        mine.start()
        mine.wait()

    for n in range(24):
        field[0, n] = jnp.zeros((8, 128), jnp.float32)

    @pl.when(jnp.logical_not(to_self & (zhi == link_hi)))
    def _():
        link_copy(0).wait_recv()

    for mu in range(4):
        scale = -0.5 / filter_radius
        if mu == 3:
            scale = scale * jnp.where(t == nt - 1, -1.0, 1.0)
        rows = [
            jnp.broadcast_to(g_in[mu * 12 + r : mu * 12 + r + 1, :], (8, 128)) for r in range(12)
        ]
        for r in range(12):
            links[mu * 18 + r] = rows[r] * scale
        for i in range(3):
            j, k = (i + 1) % 3, (i + 2) % 3
            a_re, a_im, b_re, b_im = rows[2 * j], rows[2 * j + 1], rows[6 + 2 * k], rows[7 + 2 * k]
            c_re, c_im, d_re, d_im = rows[2 * k], rows[2 * k + 1], rows[6 + 2 * j], rows[7 + 2 * j]
            re = (a_re * b_re - a_im * b_im) - (c_re * d_re - c_im * d_im)
            im = (c_re * d_im + c_im * d_re) - (a_re * b_im + a_im * b_re)
            links[mu * 18 + 12 + 2 * i] = re * scale
            links[mu * 18 + 13 + 2 * i] = im * scale

    for n in range(4):

        @pl.when(jnp.logical_not(to_self & (slot == n)))
        def _():
            pltpu.make_async_remote_copy(
                src_ref=block(stage, 0),
                dst_ref=block(psi_in, n),
                send_sem=send1.at[0],
                recv_sem=recv1.at[n],
                device_id=near[TP],
                device_id_type=MESH,
            ).wait_recv()

    for n in range(24):
        field[1, n] = psi_in[pl.ds(n, 8, stride=24), :]

    lane = lax.broadcasted_iota(jnp.int32, (8, 128), 1)
    sub = lax.broadcasted_iota(jnp.int32, (8, 128), 0)
    low = lane < 64

    def shift(value, direction, forward):
        stride = 8**direction
        position = lax.rem(lax.div(lane, stride), 8)
        inside, outside = (128 - stride, 7 * stride) if forward else (stride, 128 - 7 * stride)
        edge = position == (7 if forward else 0)
        return jnp.where(edge, pltpu.roll(value, outside, 1), pltpu.roll(value, inside, 1))

    def half_turn(value):
        return pltpu.roll(value, 64, 1)

    def step(it, carry):
        def v(n):
            return field[it + 1, n]

        def link(mu):
            return lambda row, column, part: links[mu * 18 + (row * 3 + column) * 2 + part]

        def halo(side, source, target):
            return pltpu.make_async_remote_copy(
                src_ref=source,
                dst_ref=target,
                send_sem=sendh.at[it, side],
                recv_sem=recvh.at[it, side],
                device_id=near[side],
                device_id_type=MESH,
            )

        to_t_up = halo(TP, tsend.at[it, 0], trecv.at[it, 0])
        to_t_down = halo(TM, tsend.at[it, 1], trecv.at[it, 1])
        to_k_up = halo(KP, ksend.at[it, 0], krecv.at[it, 0])
        to_k_down = halo(KM, ksend.at[it, 1], krecv.at[it, 1])
        to_s_up = halo(SP, ssend.at[it, 0], srecv.at[it, 0])
        to_s_down = halo(SM, ssend.at[it, 1], srecv.at[it, 1])

        behind = colour_mul(link(3), project(v, 3, 1.0), True)
        for n in range(12):
            tsend[it, 0, n] = behind[n]
        to_t_up.start()
        front = project(v, 3, -1.0)
        for n in range(12):
            tsend[it, 1, n] = front[n]
        to_t_down.start()

        behind = colour_mul(link(2), project(v, 2, 1.0), True)
        for m in range(6):
            a, b = behind[2 * m], behind[2 * m + 1]
            ra, rb = half_turn(a), half_turn(b)
            ksend[it, 0, m] = jnp.where(low, ra, b)
            klocal[0, 2 * m] = ra
            klocal[0, 2 * m + 1] = rb
        to_k_up.start()
        front = project(v, 2, -1.0)
        for m in range(6):
            a, b = front[2 * m], front[2 * m + 1]
            ra, rb = half_turn(a), half_turn(b)
            ksend[it, 1, m] = jnp.where(low, a, rb)
            klocal[1, 2 * m] = ra
            klocal[1, 2 * m + 1] = rb
        to_k_down.start()

        for n in range(24):
            value = v(n)
            up, down = (3, 4) if n < 12 else (7, 0)
            ssend[it, 0, n : n + 1] = value[up : up + 1]
            ssend[it, 1, n : n + 1] = value[down : down + 1]

        @pl.when(y < NY - 1)
        def _():
            to_s_up.start()

        @pl.when(y > 0)
        def _():
            to_s_down.start()

        @pl.when(y == NY - 1)
        def _():
            srecv[it, 1] = ssend[it, 0]

        @pl.when(y == 0)
        def _():
            srecv[it, 0] = ssend[it, 1] * -quark_mass

        total = [((5.0 - wall_height) / filter_radius) * v(n) for n in range(24)]
        for direction in range(2):
            front = [shift(value, direction, True) for value in project(v, direction, -1.0)]
            add_rebuilt(total, colour_mul(link(direction), front, False), direction, -1.0)
            behind = colour_mul(link(direction), project(v, direction, 1.0), True)
            add_rebuilt(total, [shift(value, direction, False) for value in behind], direction, 1.0)

        to_k_up.wait_recv()
        behind = []
        for m in range(6):
            packed = krecv[it, 0, m]
            behind.append(jnp.where(low, packed, klocal[0, 2 * m]))
            behind.append(jnp.where(low, half_turn(packed), klocal[0, 2 * m + 1]))
        add_rebuilt(total, behind, 2, 1.0)
        to_k_down.wait_recv()
        front = []
        for m in range(6):
            packed = krecv[it, 1, m]
            front.append(jnp.where(low, klocal[1, 2 * m], half_turn(packed)))
            front.append(jnp.where(low, klocal[1, 2 * m + 1], packed))
        add_rebuilt(total, colour_mul(link(2), front, False), 2, -1.0)

        @pl.when(y > 0)
        def _():
            to_s_up.wait_recv()

        @pl.when(y < NY - 1)
        def _():
            to_s_down.wait_recv()

        for n in range(24):
            value = v(n)
            back, on = pltpu.roll(value, 1, 0), pltpu.roll(value, 7, 0)
            from_low = jnp.broadcast_to(srecv[it, 0, n : n + 1], (8, 128))
            from_high = jnp.broadcast_to(srecv[it, 1, n : n + 1], (8, 128))
            if n < 12:
                inner = jnp.where(sub < 4, back, on)
                moved = jnp.where(sub == 0, from_low, jnp.where(sub == 7, from_high, inner))
            else:
                inner = jnp.where(sub < 4, on, back)
                moved = jnp.where(sub == 4, from_low, jnp.where(sub == 3, from_high, inner))
            total[n] = total[n] - (1.0 / filter_radius) * moved

        to_t_up.wait_recv()
        add_rebuilt(total, [trecv[it, 0, n] for n in range(12)], 3, 1.0)
        to_t_down.wait_recv()
        front = [trecv[it, 1, n] for n in range(12)]
        add_rebuilt(total, colour_mul(link(3), front, False), 3, -1.0)

        gain = jnp.where(it == 0, 1.0, 2.0)
        for n in range(24):
            signed = pltpu.roll(total[n], 4, 0)
            centred = (filter_center / filter_radius) * v(n)
            inner = (signed if n < 12 else -signed) - centred
            field[it + 2, n] = gain * inner - field[it, n]
        return carry

    lax.fori_loop(0, DEGREE, step, 0)

    for n in range(24):
        ostage[pl.ds(n, 8, stride=24), :] = field[DEGREE + 1, n]

    def back_copy(n):
        return pltpu.make_async_remote_copy(
            src_ref=block(ostage, n),
            dst_ref=block(o_in, x),
            send_sem=send2.at[n],
            recv_sem=recv2.at[x],
            device_id=(sources[n], t),
            device_id_type=MESH,
        )

    for n in range(4):

        @pl.when(jnp.logical_not(to_self & (slot == n)))
        def _():
            back_copy(n).start()

    @pl.when(to_self)
    def _():
        mine = pltpu.make_async_copy(block(ostage, slot), block(o_in, x), local.at[0])
        mine.start()
        mine.wait()

    for q in range(NX):

        @pl.when(jnp.logical_not(to_self & (x == q)))
        def _():
            pltpu.make_async_remote_copy(
                src_ref=block(ostage, 0),
                dst_ref=block(o_in, q),
                send_sem=send2.at[0],
                recv_sem=recv2.at[q],
                device_id=near[TP],
                device_id_type=MESH,
            ).wait_recv()

        for s in range(2):
            for b in range(3):
                row = pl.multiple_of(q * 48 + lax.rem(s + flip, 2) * 24 + b * 8, 8)
                out_ref[pl.ds((s * 24 + b * 8) * 4 + q, 8, stride=4), :] = o_in[pl.ds(row, 8), :]

    for q in range(NX):
        other = jnp.logical_not(to_self & (x == q))

        @pl.when(other)
        def _():
            out_copy(q).wait_send()

        @pl.when(other & gives_links)
        def _():
            link_copy(q).wait_send()

    def sent(it, carry):
        def left(side, source, target):
            pltpu.make_async_remote_copy(
                src_ref=source,
                dst_ref=target,
                send_sem=sendh.at[it, side],
                recv_sem=recvh.at[it, side],
                device_id=near[side],
                device_id_type=MESH,
            ).wait_send()

        left(TP, tsend.at[it, 0], trecv.at[it, 0])
        left(TM, tsend.at[it, 1], trecv.at[it, 1])
        left(KP, ksend.at[it, 0], krecv.at[it, 0])
        left(KM, ksend.at[it, 1], krecv.at[it, 1])

        @pl.when(y < NY - 1)
        def _():
            left(SP, ssend.at[it, 0], srecv.at[it, 0])

        @pl.when(y > 0)
        def _():
            left(SM, ssend.at[it, 1], srecv.at[it, 1])

        return carry

    lax.fori_loop(0, DEGREE, sent, 0)

    for n in range(4):

        @pl.when(jnp.logical_not(to_self & (slot == n)))
        def _():
            back_copy(n).wait_send()


def solution(mesh):
    nlo = mesh.shape["space"] // (NX * NC)
    vmem = pl.BlockSpec(memory_space=pltpu.VMEM)

    def f32(*shape):
        return pltpu.VMEM(shape, jnp.float32)

    dma = pltpu.SemaphoreType.DMA

    def on_device(spinor, gauge_links):
        out = pl.pallas_call(
            functools.partial(kernel, nlo),
            out_shape=jax.ShapeDtypeStruct((192, 128), jnp.float32),
            in_specs=[vmem, vmem],
            out_specs=vmem,
            scratch_shapes=[
                f32(192, 128),
                f32(192, 128),
                f32(192, 128),
                f32(48, 128),
                f32(72, 8, 128),
                f32(DEGREE + 2, 24, 8, 128),
                f32(DEGREE, 2, 12, 8, 128),
                f32(DEGREE, 2, 12, 8, 128),
                f32(DEGREE, 2, 6, 8, 128),
                f32(DEGREE, 2, 6, 8, 128),
                f32(2, 12, 8, 128),
                f32(DEGREE, 2, 24, 128),
                f32(DEGREE, 2, 24, 128),
                f32(192, 128),
                f32(192, 128),
                dma((4,)),
                dma((4,)),
                dma((4,)),
                dma((1,)),
                dma((DEGREE, 6)),
                dma((DEGREE, 6)),
                dma((4,)),
                dma((4,)),
                dma((2,)),
            ],
            compiler_params=pltpu.CompilerParams(
                collective_id=0, has_side_effects=True, vmem_limit_bytes=16 * 2**20
            ),
        )(spinor.reshape(192, 128), gauge_links.reshape(288, 128))
        return out.reshape(2, 24, 1, 512)

    return jax.shard_map(
        on_device,
        mesh=mesh,
        in_specs=(P("fifth", None, "space", None), P(None, None, "space", None)),
        out_specs=P("fifth", None, "space", None),
        check_vma=False,
    )
```

```python
import functools

import jax
import jax.numpy as jnp
from jax import lax
from jax.experimental import pallas as pl
from jax.experimental.pallas import tpu as pltpu
from jax.sharding import PartitionSpec as P

MESH = pl.DeviceIdType.MESH
wall_height = 1.8
quark_mass = 0.1
filter_center = 0.5
filter_radius = 8.0
DEGREE = 4
gamma_block = (((1, 1), (0, 1)), ((1, 2), (0, 0)), ((0, 1), (1, 3)), ((0, 0), (1, 0)))
gamma_adjoint = (((1, 3), (0, 3)), ((1, 0), (0, 2)), ((0, 3), (1, 1)), ((0, 0), (1, 0)))
NX, NY, NHI, NC = 4, 4, 4, 2
Z_OFFSET = 28
TP, TM, KP, KM, SP, SM = range(6)


def unit_part(quarter, part):
    if part == 0:
        return ((1.0, 0), (-1.0, 1), (-1.0, 0), (1.0, 1))[quarter]
    return ((1.0, 1), (1.0, 0), (-1.0, 1), (-1.0, 0))[quarter]


def plus(value, sign, term):
    return value + term if sign > 0 else value - term


def comp(spin, colour, part):
    return (spin * 3 + colour) * 2 + part


def project(field, direction, parity):
    half = []
    for row in range(2):
        source, quarter = gamma_block[direction][row]
        for colour in range(3):
            for part in range(2):
                sign, other = unit_part(quarter, part)
                half.append(
                    plus(field(comp(row, colour, part)), parity * sign, field(comp(2 + source, colour, other)))
                )
    return half


def add_rebuilt(total, half, direction, parity):
    for row in range(2):
        source, quarter = gamma_adjoint[direction][row]
        for colour in range(3):
            for part in range(2):
                n = comp(row, colour, part)
                total[n] = total[n] + half[n]
                sign, other = unit_part(quarter, part)
                m = comp(2 + row, colour, part)
                total[m] = plus(total[m], parity * sign, half[comp(source, colour, other)])


def colour_mul(link, half, dagger):
    result = [None] * 12
    for row in range(3):
        for column in range(3):
            if dagger:
                u_re, u_im, sign = link(column, row, 0), link(column, row, 1), -1.0
            else:
                u_re, u_im, sign = link(row, column, 0), link(row, column, 1), 1.0
            for spin in range(2):
                h_re, h_im = half[comp(spin, column, 0)], half[comp(spin, column, 1)]
                re = plus(u_re * h_re, -sign, u_im * h_im)
                im = plus(u_re * h_im, sign, u_im * h_re)
                r, i = comp(spin, row, 0), comp(spin, row, 1)
                result[r] = re if column == 0 else result[r] + re
                result[i] = im if column == 0 else result[i] + im
    return result


def kernel(
    nlo,
    sp_hbm,
    g_hbm,
    out_ref,
    sp_ref,
    g_ref,
    stage,
    gstage,
    psi_in,
    g_in,
    links,
    field,
    tsend,
    trecv,
    ksend,
    krecv,
    klocal,
    ssend,
    srecv,
    ostage,
    o_in,
    send1,
    recv1,
    sendg,
    recvg,
    sendh,
    recvh,
    send2,
    recv2,
    local,
):
    nz = NHI * nlo
    nt = nz * NC
    f = lax.axis_index("fifth")
    p = lax.axis_index("space")
    y, zhi = lax.div(f, NHI), lax.rem(f, NHI)
    zlo, x, c = lax.div(p, NX * NC), lax.rem(lax.div(p, NC), NX), lax.rem(p, NC)
    z = zhi * nlo + zlo

    def device(dx, dy, dz, dc):
        return (dy * NHI + lax.div(dz, nlo), lax.rem(dz, nlo) * (NX * NC) + dx * NC + dc)

    z_to = lax.rem(lax.div(p, NC) + Z_OFFSET, nz)
    upper = f >= 8
    folded = jnp.where(upper, 15 - f, f)
    y_to = lax.rem(NY - lax.div(folded, 2), NY)
    slot = jnp.where(upper, 2, 0) + lax.rem(folded, 2)
    flip = jnp.where(upper, 1, 0)
    ahead = lax.rem(z_to - zlo + nz, nz)
    gives_links = zhi == lax.rem(lax.div(ahead + nlo // 2, nlo), NHI)
    to_self = (y_to == y) & (z_to == z)
    t = lax.rem(z + nz - Z_OFFSET % nz, nz) * NC + c
    seg = lax.rem(NY - y, NY)
    sources = (2 * seg, 2 * seg + 1, 15 - 2 * seg, 14 - 2 * seg)
    ahead_me = lax.rem(z - lax.div(t, NX * NC) + nz, nz)
    link_hi = lax.rem(lax.div(ahead_me + nlo // 2, nlo), NHI)

    t_up, t_down = lax.rem(t + 1, nt), lax.rem(t + nt - 1, nt)
    near = {
        TP: device(x, y, lax.rem(lax.div(t_up, NC) + Z_OFFSET, nz), lax.rem(t_up, NC)),
        TM: device(x, y, lax.rem(lax.div(t_down, NC) + Z_OFFSET, nz), lax.rem(t_down, NC)),
        KP: device(lax.rem(x + 1, NX), y, z, c),
        KM: device(lax.rem(x + NX - 1, NX), y, z, c),
        SP: device(x, lax.rem(y + NY - 1, NY), z, c),
        SM: device(x, lax.rem(y + 1, NY), z, c),
    }

    barrier = pltpu.get_barrier_semaphore()

    def greet(device_id):
        pl.semaphore_signal(barrier, inc=1, device_id=device_id, device_id_type=MESH)

    for n in range(4):

        @pl.when(jnp.logical_not(to_self & (slot == n)))
        def _():
            greet((sources[n], t))

    for side in (TP, TM, KP, KM):
        greet(near[side])

    @pl.when(seg < NY - 1)
    def _():
        greet(near[SP])

    @pl.when(seg > 0)
    def _():
        greet(near[SM])

    for source, target, sem in ((sp_hbm, sp_ref, 2), (g_hbm, g_ref, 3)):
        pltpu.make_async_copy(source, target, local.at[sem]).start()
    pltpu.make_async_copy(sp_hbm, sp_ref, local.at[2]).wait()
    pltpu.make_async_copy(g_hbm, g_ref, local.at[3]).wait()

    for q in range(NX):
        for s in range(2):
            for b in range(3):
                row = pl.multiple_of(q * 48 + lax.rem(s + flip, 2) * 24 + b * 8, 8)
                stage[pl.ds(row, 8), :] = sp_ref[pl.ds((s * 24 + b * 8) * 4 + q, 8, stride=4), :]
        for mu in range(4):
            first = g_ref[pl.ds(mu * 72 + q, 8, stride=4), :]
            gstage[q * 48 + mu * 12 : q * 48 + mu * 12 + 8, :] = first
            last = g_ref[pl.ds(mu * 72 + 32 + q, 4, stride=4), :]
            gstage[q * 48 + mu * 12 + 8 : q * 48 + mu * 12 + 12, :] = last

    count = 8 - jnp.where(to_self, 1, 0) + jnp.where(seg > 0, 1, 0) + jnp.where(seg < NY - 1, 1, 0)
    pl.semaphore_wait(barrier, count)

    def block(ref, n):
        start = n * 48
        return ref.at[pl.ds(start if isinstance(n, int) else pl.multiple_of(start, 8), 48), :]

    def out_copy(q):
        return pltpu.make_async_remote_copy(
            src_ref=block(stage, q),
            dst_ref=block(psi_in, slot),
            send_sem=send1.at[q],
            recv_sem=recv1.at[slot],
            device_id=device(q, y_to, z_to, c),
            device_id_type=MESH,
        )

    def link_copy(q):
        return pltpu.make_async_remote_copy(
            src_ref=block(gstage, q),
            dst_ref=g_in,
            send_sem=sendg.at[q],
            recv_sem=recvg.at[0],
            device_id=device(q, y_to, z_to, c),
            device_id_type=MESH,
        )

    for q in range(NX):
        other = jnp.logical_not(to_self & (x == q))

        @pl.when(other)
        def _():
            out_copy(q).start()

        @pl.when(other & gives_links)
        def _():
            link_copy(q).start()

    @pl.when(to_self)
    def _():
        mine = pltpu.make_async_copy(block(stage, x), block(psi_in, slot), local.at[0])
        mine.start()
        mine.wait()

    @pl.when(to_self & gives_links)
    def _():
        mine = pltpu.make_async_copy(block(gstage, x), g_in, local.at[1])
        mine.start()
        mine.wait()

    for n in range(24):
        field[0, n] = jnp.zeros((8, 128), jnp.float32)

    @pl.when(jnp.logical_not(to_self & (zhi == link_hi)))
    def _():
        link_copy(0).wait_recv()

    for mu in range(4):
        scale = -0.5 / filter_radius
        if mu == 3:
            scale = scale * jnp.where(t == nt - 1, -1.0, 1.0)
        rows = [
            jnp.broadcast_to(g_in[mu * 12 + r : mu * 12 + r + 1, :], (8, 128)) for r in range(12)
        ]
        for r in range(12):
            links[mu * 18 + r] = rows[r] * scale
        for i in range(3):
            j, k = (i + 1) % 3, (i + 2) % 3
            a_re, a_im, b_re, b_im = rows[2 * j], rows[2 * j + 1], rows[6 + 2 * k], rows[7 + 2 * k]
            c_re, c_im, d_re, d_im = rows[2 * k], rows[2 * k + 1], rows[6 + 2 * j], rows[7 + 2 * j]
            re = (a_re * b_re - a_im * b_im) - (c_re * d_re - c_im * d_im)
            im = (c_re * d_im + c_im * d_re) - (a_re * b_im + a_im * b_re)
            links[mu * 18 + 12 + 2 * i] = re * scale
            links[mu * 18 + 13 + 2 * i] = im * scale

    for n in range(4):

        @pl.when(jnp.logical_not(to_self & (slot == n)))
        def _():
            pltpu.make_async_remote_copy(
                src_ref=block(stage, 0),
                dst_ref=block(psi_in, n),
                send_sem=send1.at[0],
                recv_sem=recv1.at[n],
                device_id=near[TP],
                device_id_type=MESH,
            ).wait_recv()

    for n in range(24):
        field[1, n] = psi_in[pl.ds(n, 8, stride=24), :]

    lane = lax.broadcasted_iota(jnp.int32, (8, 128), 1)
    sub = lax.broadcasted_iota(jnp.int32, (8, 128), 0)
    low = lane < 64

    def shift(value, direction, forward):
        stride = 8**direction
        position = lax.rem(lax.div(lane, stride), 8)
        inside, outside = (128 - stride, 7 * stride) if forward else (stride, 128 - 7 * stride)
        edge = position == (7 if forward else 0)
        return jnp.where(edge, pltpu.roll(value, outside, 1), pltpu.roll(value, inside, 1))

    def half_turn(value):
        return pltpu.roll(value, 64, 1)

    def step(it, carry):
        def v(n):
            return field[it + 1, n]

        def link(mu):
            return lambda row, column, part: links[mu * 18 + (row * 3 + column) * 2 + part]

        def halo(side, source, target):
            return pltpu.make_async_remote_copy(
                src_ref=source,
                dst_ref=target,
                send_sem=sendh.at[it, side],
                recv_sem=recvh.at[it, side],
                device_id=near[side],
                device_id_type=MESH,
            )

        to_t_up = halo(TP, tsend.at[it, 0], trecv.at[it, 0])
        to_t_down = halo(TM, tsend.at[it, 1], trecv.at[it, 1])
        to_k_up = halo(KP, ksend.at[it, 0], krecv.at[it, 0])
        to_k_down = halo(KM, ksend.at[it, 1], krecv.at[it, 1])
        to_s_up = halo(SP, ssend.at[it, 0], srecv.at[it, 0])
        to_s_down = halo(SM, ssend.at[it, 1], srecv.at[it, 1])

        behind = colour_mul(link(3), project(v, 3, 1.0), True)
        for n in range(12):
            tsend[it, 0, n] = behind[n]
        to_t_up.start()
        front = project(v, 3, -1.0)
        for n in range(12):
            tsend[it, 1, n] = front[n]
        to_t_down.start()

        behind = colour_mul(link(2), project(v, 2, 1.0), True)
        for m in range(6):
            a, b = behind[2 * m], behind[2 * m + 1]
            ra, rb = half_turn(a), half_turn(b)
            ksend[it, 0, m] = jnp.where(low, ra, b)
            klocal[0, 2 * m] = ra
            klocal[0, 2 * m + 1] = rb
        to_k_up.start()
        front = project(v, 2, -1.0)
        for m in range(6):
            a, b = front[2 * m], front[2 * m + 1]
            ra, rb = half_turn(a), half_turn(b)
            ksend[it, 1, m] = jnp.where(low, a, rb)
            klocal[1, 2 * m] = ra
            klocal[1, 2 * m + 1] = rb
        to_k_down.start()

        for n in range(24):
            value = v(n)
            up, down = (3, 4) if n < 12 else (7, 0)
            ssend[it, 0, n : n + 1] = value[up : up + 1]
            ssend[it, 1, n : n + 1] = value[down : down + 1]

        @pl.when(seg < NY - 1)
        def _():
            to_s_up.start()

        @pl.when(seg > 0)
        def _():
            to_s_down.start()

        @pl.when(seg == NY - 1)
        def _():
            srecv[it, 1] = ssend[it, 0]

        @pl.when(seg == 0)
        def _():
            srecv[it, 0] = ssend[it, 1] * -quark_mass

        total = [((5.0 - wall_height) / filter_radius) * v(n) for n in range(24)]
        for direction in range(2):
            front = [shift(value, direction, True) for value in project(v, direction, -1.0)]
            add_rebuilt(total, colour_mul(link(direction), front, False), direction, -1.0)
            behind = colour_mul(link(direction), project(v, direction, 1.0), True)
            add_rebuilt(total, [shift(value, direction, False) for value in behind], direction, 1.0)

        to_k_up.wait_recv()
        behind = []
        for m in range(6):
            packed = krecv[it, 0, m]
            behind.append(jnp.where(low, packed, klocal[0, 2 * m]))
            behind.append(jnp.where(low, half_turn(packed), klocal[0, 2 * m + 1]))
        add_rebuilt(total, behind, 2, 1.0)
        to_k_down.wait_recv()
        front = []
        for m in range(6):
            packed = krecv[it, 1, m]
            front.append(jnp.where(low, klocal[1, 2 * m], half_turn(packed)))
            front.append(jnp.where(low, klocal[1, 2 * m + 1], packed))
        add_rebuilt(total, colour_mul(link(2), front, False), 2, -1.0)

        @pl.when(seg > 0)
        def _():
            to_s_up.wait_recv()

        @pl.when(seg < NY - 1)
        def _():
            to_s_down.wait_recv()

        for n in range(24):
            value = v(n)
            back, on = pltpu.roll(value, 1, 0), pltpu.roll(value, 7, 0)
            from_low = jnp.broadcast_to(srecv[it, 0, n : n + 1], (8, 128))
            from_high = jnp.broadcast_to(srecv[it, 1, n : n + 1], (8, 128))
            if n < 12:
                inner = jnp.where(sub < 4, back, on)
                moved = jnp.where(sub == 0, from_low, jnp.where(sub == 7, from_high, inner))
            else:
                inner = jnp.where(sub < 4, on, back)
                moved = jnp.where(sub == 4, from_low, jnp.where(sub == 3, from_high, inner))
            total[n] = total[n] - (1.0 / filter_radius) * moved

        to_t_up.wait_recv()
        add_rebuilt(total, [trecv[it, 0, n] for n in range(12)], 3, 1.0)
        to_t_down.wait_recv()
        front = [trecv[it, 1, n] for n in range(12)]
        add_rebuilt(total, colour_mul(link(3), front, False), 3, -1.0)

        gain = jnp.where(it == 0, 1.0, 2.0)
        for n in range(24):
            signed = pltpu.roll(total[n], 4, 0)
            centred = (filter_center / filter_radius) * v(n)
            inner = (signed if n < 12 else -signed) - centred
            field[it + 2, n] = gain * inner - field[it, n]
        return carry

    lax.fori_loop(0, DEGREE, step, 0)

    for n in range(24):
        ostage[pl.ds(n, 8, stride=24), :] = field[DEGREE + 1, n]

    def back_copy(n):
        return pltpu.make_async_remote_copy(
            src_ref=block(ostage, n),
            dst_ref=block(o_in, x),
            send_sem=send2.at[n],
            recv_sem=recv2.at[x],
            device_id=(sources[n], t),
            device_id_type=MESH,
        )

    for early in (True, False):
        for n in range(4):
            first = (lax.rem(sources[n], NHI) < 2) if early else (lax.rem(sources[n], NHI) >= 2)

            @pl.when(jnp.logical_not(to_self & (slot == n)) & first)
            def _():
                back_copy(n).start()

        if early:
            for n in range(4):

                @pl.when(jnp.logical_not(to_self & (slot == n)) & (lax.rem(sources[n], NHI) < 2))
                def _():
                    back_copy(n).wait_send()

    @pl.when(to_self)
    def _():
        mine = pltpu.make_async_copy(block(ostage, slot), block(o_in, x), local.at[0])
        mine.start()
        mine.wait()

    for q in range(NX):

        @pl.when(jnp.logical_not(to_self & (x == q)))
        def _():
            pltpu.make_async_remote_copy(
                src_ref=block(ostage, 0),
                dst_ref=block(o_in, q),
                send_sem=send2.at[0],
                recv_sem=recv2.at[q],
                device_id=near[TP],
                device_id_type=MESH,
            ).wait_recv()

        for s in range(2):
            for b in range(3):
                row = pl.multiple_of(q * 48 + lax.rem(s + flip, 2) * 24 + b * 8, 8)
                out_ref[pl.ds((s * 24 + b * 8) * 4 + q, 8, stride=4), :] = o_in[pl.ds(row, 8), :]

    for q in range(NX):
        other = jnp.logical_not(to_self & (x == q))

        @pl.when(other)
        def _():
            out_copy(q).wait_send()

        @pl.when(other & gives_links)
        def _():
            link_copy(q).wait_send()

    def sent(it, carry):
        def left(side, source, target):
            pltpu.make_async_remote_copy(
                src_ref=source,
                dst_ref=target,
                send_sem=sendh.at[it, side],
                recv_sem=recvh.at[it, side],
                device_id=near[side],
                device_id_type=MESH,
            ).wait_send()

        left(TP, tsend.at[it, 0], trecv.at[it, 0])
        left(TM, tsend.at[it, 1], trecv.at[it, 1])
        left(KP, ksend.at[it, 0], krecv.at[it, 0])
        left(KM, ksend.at[it, 1], krecv.at[it, 1])

        @pl.when(seg < NY - 1)
        def _():
            left(SP, ssend.at[it, 0], srecv.at[it, 0])

        @pl.when(seg > 0)
        def _():
            left(SM, ssend.at[it, 1], srecv.at[it, 1])

        return carry

    lax.fori_loop(0, DEGREE, sent, 0)

    for n in range(4):

        @pl.when(jnp.logical_not(to_self & (slot == n)) & (lax.rem(sources[n], NHI) >= 2))
        def _():
            back_copy(n).wait_send()


def solution(mesh):
    nlo = mesh.shape["space"] // (NX * NC)
    vmem = pl.BlockSpec(memory_space=pltpu.VMEM)

    def f32(*shape):
        return pltpu.VMEM(shape, jnp.float32)

    dma = pltpu.SemaphoreType.DMA

    def on_device(spinor, gauge_links):
        out = pl.pallas_call(
            functools.partial(kernel, nlo),
            out_shape=jax.ShapeDtypeStruct((192, 128), jnp.float32),
            in_specs=[pl.BlockSpec(memory_space=pl.ANY)] * 2,
            out_specs=vmem,
            scratch_shapes=[
                f32(192, 128),
                f32(288, 128),
                f32(192, 128),
                f32(192, 128),
                f32(192, 128),
                f32(48, 128),
                f32(72, 8, 128),
                f32(DEGREE + 2, 24, 8, 128),
                f32(DEGREE, 2, 12, 8, 128),
                f32(DEGREE, 2, 12, 8, 128),
                f32(DEGREE, 2, 6, 8, 128),
                f32(DEGREE, 2, 6, 8, 128),
                f32(2, 12, 8, 128),
                f32(DEGREE, 2, 24, 128),
                f32(DEGREE, 2, 24, 128),
                f32(192, 128),
                f32(192, 128),
                dma((4,)),
                dma((4,)),
                dma((4,)),
                dma((1,)),
                dma((DEGREE, 6)),
                dma((DEGREE, 6)),
                dma((4,)),
                dma((4,)),
                dma((4,)),
            ],
            compiler_params=pltpu.CompilerParams(
                collective_id=0, has_side_effects=True, vmem_limit_bytes=60 * 2**20
            ),
        )(spinor.reshape(192, 128), gauge_links.reshape(288, 128))
        return out.reshape(2, 24, 1, 512)

    return jax.shard_map(
        on_device,
        mesh=mesh,
        in_specs=(P("fifth", None, "space", None), P(None, None, "space", None)),
        out_specs=P("fifth", None, "space", None),
        check_vma=False,
    )
```

```python
import functools

import jax
import jax.numpy as jnp
from jax import lax
from jax.experimental import pallas as pl
from jax.experimental.pallas import tpu as pltpu
from jax.sharding import PartitionSpec as P

MESH = pl.DeviceIdType.MESH
wall_height = 1.8
quark_mass = 0.1
filter_center = 0.5
filter_radius = 8.0
DEGREE = 4
gamma_block = (((1, 1), (0, 1)), ((1, 2), (0, 0)), ((0, 1), (1, 3)), ((0, 0), (1, 0)))
gamma_adjoint = (((1, 3), (0, 3)), ((1, 0), (0, 2)), ((0, 3), (1, 1)), ((0, 0), (1, 0)))
NX, NY, NHI, NC = 4, 4, 4, 2
Z_OFFSET = 7
Z_SIGN = -1
ROUNDS = 3
TP, TM, KP, KM, SP, SM = range(6)


def unit_part(quarter, part):
    if part == 0:
        return ((1.0, 0), (-1.0, 1), (-1.0, 0), (1.0, 1))[quarter]
    return ((1.0, 1), (1.0, 0), (-1.0, 1), (-1.0, 0))[quarter]


def plus(value, sign, term):
    return value + term if sign > 0 else value - term


def comp(spin, colour, part):
    return (spin * 3 + colour) * 2 + part


def project(field, direction, parity):
    half = []
    for row in range(2):
        source, quarter = gamma_block[direction][row]
        for colour in range(3):
            for part in range(2):
                sign, other = unit_part(quarter, part)
                half.append(
                    plus(field(comp(row, colour, part)), parity * sign, field(comp(2 + source, colour, other)))
                )
    return half


def add_rebuilt(total, half, direction, parity):
    for row in range(2):
        source, quarter = gamma_adjoint[direction][row]
        for colour in range(3):
            for part in range(2):
                n = comp(row, colour, part)
                total[n] = total[n] + half[n]
                sign, other = unit_part(quarter, part)
                m = comp(2 + row, colour, part)
                total[m] = plus(total[m], parity * sign, half[comp(source, colour, other)])


def colour_mul(link, half, dagger):
    result = [None] * 12
    for row in range(3):
        for column in range(3):
            if dagger:
                u_re, u_im, sign = link(column, row, 0), link(column, row, 1), -1.0
            else:
                u_re, u_im, sign = link(row, column, 0), link(row, column, 1), 1.0
            for spin in range(2):
                h_re, h_im = half[comp(spin, column, 0)], half[comp(spin, column, 1)]
                re = plus(u_re * h_re, -sign, u_im * h_im)
                im = plus(u_re * h_im, sign, u_im * h_re)
                r, i = comp(spin, row, 0), comp(spin, row, 1)
                result[r] = re if column == 0 else result[r] + re
                result[i] = im if column == 0 else result[i] + im
    return result


def kernel(
    nlo,
    sp_hbm,
    g_hbm,
    out_ref,
    sp_ref,
    g_ref,
    stage,
    gstage,
    psi_in,
    g_in,
    links,
    field,
    tsend,
    trecv,
    ksend,
    krecv,
    klocal,
    ssend,
    srecv,
    ostage,
    o_in,
    send1,
    recv1,
    sendg,
    recvg,
    sendh,
    recvh,
    send2,
    recv2,
    local,
    phase,
):
    nz = NHI * nlo
    nt = nz * NC
    f = lax.axis_index("fifth")
    p = lax.axis_index("space")
    y, zhi = lax.div(f, NHI), lax.rem(f, NHI)
    zlo, x, c = lax.div(p, NX * NC), lax.rem(lax.div(p, NC), NX), lax.rem(p, NC)
    z = zhi * nlo + zlo

    def device(dx, dy, dz, dc):
        return (dy * NHI + lax.div(dz, nlo), lax.rem(dz, nlo) * (NX * NC) + dx * NC + dc)

    def z_of(time):
        return lax.rem(Z_SIGN * lax.div(time, NC) + Z_OFFSET + nz, nz)

    z_to = z_of(p)
    upper = f >= 8
    folded = jnp.where(upper, 15 - f, f)
    y_to = lax.rem(NY - lax.div(folded, 2), NY)
    slot = jnp.where(upper, 2, 0) + lax.rem(folded, 2)
    flip = jnp.where(upper, 1, 0)
    ahead = lax.rem(z_to - zlo + nz, nz)
    gives_links = zhi == lax.rem(lax.div(ahead + nlo // 2, nlo), NHI)
    to_self = (y_to == y) & (z_to == z)
    t = lax.rem(Z_SIGN * (z - Z_OFFSET) + nz + nz, nz) * NC + c
    seg = lax.rem(NY - y, NY)
    sources = (2 * seg, 2 * seg + 1, 15 - 2 * seg, 14 - 2 * seg)
    ahead_me = lax.rem(z - lax.div(t, NX * NC) + nz, nz)
    link_hi = lax.rem(lax.div(ahead_me + nlo // 2, nlo), NHI)

    t_up, t_down = lax.rem(t + 1, nt), lax.rem(t + nt - 1, nt)
    near = {
        TP: device(x, y, z_of(t_up), lax.rem(t_up, NC)),
        TM: device(x, y, z_of(t_down), lax.rem(t_down, NC)),
        KP: device(lax.rem(x + 1, NX), y, z, c),
        KM: device(lax.rem(x + NX - 1, NX), y, z, c),
        SP: device(x, lax.rem(y + NY - 1, NY), z, c),
        SM: device(x, lax.rem(y + 1, NY), z, c),
    }

    barrier = pltpu.get_barrier_semaphore()

    def greet(device_id):
        pl.semaphore_signal(barrier, inc=1, device_id=device_id, device_id_type=MESH)

    for n in range(4):

        @pl.when(jnp.logical_not(to_self & (slot == n)))
        def _():
            greet((sources[n], t))

    for side in (TP, TM, KP, KM):
        greet(near[side])

    @pl.when(seg < NY - 1)
    def _():
        greet(near[SP])

    @pl.when(seg > 0)
    def _():
        greet(near[SM])

    for source, target, sem in ((sp_hbm, sp_ref, 2), (g_hbm, g_ref, 3)):
        pltpu.make_async_copy(source, target, local.at[sem]).start()
    pltpu.make_async_copy(sp_hbm, sp_ref, local.at[2]).wait()
    pltpu.make_async_copy(g_hbm, g_ref, local.at[3]).wait()

    for q in range(NX):
        for s in range(2):
            for b in range(3):
                row = pl.multiple_of(q * 48 + lax.rem(s + flip, 2) * 24 + b * 8, 8)
                stage[pl.ds(row, 8), :] = sp_ref[pl.ds((s * 24 + b * 8) * 4 + q, 8, stride=4), :]
        for mu in range(4):
            first = g_ref[pl.ds(mu * 72 + q, 8, stride=4), :]
            gstage[q * 48 + mu * 12 : q * 48 + mu * 12 + 8, :] = first
            last = g_ref[pl.ds(mu * 72 + 32 + q, 4, stride=4), :]
            gstage[q * 48 + mu * 12 + 8 : q * 48 + mu * 12 + 12, :] = last

    count = 8 - jnp.where(to_self, 1, 0) + jnp.where(seg > 0, 1, 0) + jnp.where(seg < NY - 1, 1, 0)
    pl.semaphore_wait(barrier, count)

    def block(ref, n):
        start = n * 48
        return ref.at[pl.ds(start if isinstance(n, int) else pl.multiple_of(start, 8), 48), :]

    def out_copy(q):
        return pltpu.make_async_remote_copy(
            src_ref=block(stage, q),
            dst_ref=block(psi_in, slot),
            send_sem=send1.at[q],
            recv_sem=recv1.at[slot],
            device_id=device(q, y_to, z_to, c),
            device_id_type=MESH,
        )

    def link_copy(q):
        return pltpu.make_async_remote_copy(
            src_ref=block(gstage, q),
            dst_ref=g_in,
            send_sem=sendg.at[q],
            recv_sem=recvg.at[0],
            device_id=device(q, y_to, z_to, c),
            device_id_type=MESH,
        )

    for q in range(NX):
        other = jnp.logical_not(to_self & (x == q))

        @pl.when(other)
        def _():
            out_copy(q).start()

        @pl.when(other & gives_links)
        def _():
            link_copy(q).start()

    @pl.when(to_self)
    def _():
        mine = pltpu.make_async_copy(block(stage, x), block(psi_in, slot), local.at[0])
        mine.start()
        mine.wait()

    @pl.when(to_self & gives_links)
    def _():
        mine = pltpu.make_async_copy(block(gstage, x), g_in, local.at[1])
        mine.start()
        mine.wait()

    for n in range(24):
        field[0, n] = jnp.zeros((8, 128), jnp.float32)

    @pl.when(jnp.logical_not(to_self & (zhi == link_hi)))
    def _():
        link_copy(0).wait_recv()

    for mu in range(4):
        scale = -0.5 / filter_radius
        if mu == 3:
            scale = scale * jnp.where(t == nt - 1, -1.0, 1.0)
        rows = [
            jnp.broadcast_to(g_in[mu * 12 + r : mu * 12 + r + 1, :], (8, 128)) for r in range(12)
        ]
        for r in range(12):
            links[mu * 18 + r] = rows[r] * scale
        for i in range(3):
            j, k = (i + 1) % 3, (i + 2) % 3
            a_re, a_im, b_re, b_im = rows[2 * j], rows[2 * j + 1], rows[6 + 2 * k], rows[7 + 2 * k]
            c_re, c_im, d_re, d_im = rows[2 * k], rows[2 * k + 1], rows[6 + 2 * j], rows[7 + 2 * j]
            re = (a_re * b_re - a_im * b_im) - (c_re * d_re - c_im * d_im)
            im = (c_re * d_im + c_im * d_re) - (a_re * b_im + a_im * b_re)
            links[mu * 18 + 12 + 2 * i] = re * scale
            links[mu * 18 + 13 + 2 * i] = im * scale

    for n in range(4):

        @pl.when(jnp.logical_not(to_self & (slot == n)))
        def _():
            pltpu.make_async_remote_copy(
                src_ref=block(stage, 0),
                dst_ref=block(psi_in, n),
                send_sem=send1.at[0],
                recv_sem=recv1.at[n],
                device_id=near[TP],
                device_id_type=MESH,
            ).wait_recv()

    for n in range(24):
        field[1, n] = psi_in[pl.ds(n, 8, stride=24), :]

    lane = lax.broadcasted_iota(jnp.int32, (8, 128), 1)
    sub = lax.broadcasted_iota(jnp.int32, (8, 128), 0)
    low = lane < 64

    def shift(value, direction, forward):
        stride = 8**direction
        position = lax.rem(lax.div(lane, stride), 8)
        inside, outside = (128 - stride, 7 * stride) if forward else (stride, 128 - 7 * stride)
        edge = position == (7 if forward else 0)
        return jnp.where(edge, pltpu.roll(value, outside, 1), pltpu.roll(value, inside, 1))

    def half_turn(value):
        return pltpu.roll(value, 64, 1)

    def step(it, carry):
        def v(n):
            return field[it + 1, n]

        def link(mu):
            return lambda row, column, part: links[mu * 18 + (row * 3 + column) * 2 + part]

        def halo(side, source, target):
            return pltpu.make_async_remote_copy(
                src_ref=source,
                dst_ref=target,
                send_sem=sendh.at[it, side],
                recv_sem=recvh.at[it, side],
                device_id=near[side],
                device_id_type=MESH,
            )

        to_t_up = halo(TP, tsend.at[it, 0], trecv.at[it, 0])
        to_t_down = halo(TM, tsend.at[it, 1], trecv.at[it, 1])
        to_k_up = halo(KP, ksend.at[it, 0], krecv.at[it, 0])
        to_k_down = halo(KM, ksend.at[it, 1], krecv.at[it, 1])
        to_s_up = halo(SP, ssend.at[it, 0], srecv.at[it, 0])
        to_s_down = halo(SM, ssend.at[it, 1], srecv.at[it, 1])

        behind = colour_mul(link(3), project(v, 3, 1.0), True)
        for n in range(12):
            tsend[it, 0, n] = behind[n]
        to_t_up.start()
        front = project(v, 3, -1.0)
        for n in range(12):
            tsend[it, 1, n] = front[n]
        to_t_down.start()

        behind = colour_mul(link(2), project(v, 2, 1.0), True)
        for m in range(6):
            a, b = behind[2 * m], behind[2 * m + 1]
            ra, rb = half_turn(a), half_turn(b)
            ksend[it, 0, m] = jnp.where(low, ra, b)
            klocal[0, 2 * m] = ra
            klocal[0, 2 * m + 1] = rb
        to_k_up.start()
        front = project(v, 2, -1.0)
        for m in range(6):
            a, b = front[2 * m], front[2 * m + 1]
            ra, rb = half_turn(a), half_turn(b)
            ksend[it, 1, m] = jnp.where(low, a, rb)
            klocal[1, 2 * m] = ra
            klocal[1, 2 * m + 1] = rb
        to_k_down.start()

        for n in range(24):
            value = v(n)
            up, down = (3, 4) if n < 12 else (7, 0)
            ssend[it, 0, n : n + 1] = value[up : up + 1]
            ssend[it, 1, n : n + 1] = value[down : down + 1]

        @pl.when(seg < NY - 1)
        def _():
            to_s_up.start()

        @pl.when(seg > 0)
        def _():
            to_s_down.start()

        @pl.when(seg == NY - 1)
        def _():
            srecv[it, 1] = ssend[it, 0]

        @pl.when(seg == 0)
        def _():
            srecv[it, 0] = ssend[it, 1] * -quark_mass

        total = [((5.0 - wall_height) / filter_radius) * v(n) for n in range(24)]
        for direction in range(2):
            front = [shift(value, direction, True) for value in project(v, direction, -1.0)]
            add_rebuilt(total, colour_mul(link(direction), front, False), direction, -1.0)
            behind = colour_mul(link(direction), project(v, direction, 1.0), True)
            add_rebuilt(total, [shift(value, direction, False) for value in behind], direction, 1.0)

        to_k_up.wait_recv()
        behind = []
        for m in range(6):
            packed = krecv[it, 0, m]
            behind.append(jnp.where(low, packed, klocal[0, 2 * m]))
            behind.append(jnp.where(low, half_turn(packed), klocal[0, 2 * m + 1]))
        add_rebuilt(total, behind, 2, 1.0)
        to_k_down.wait_recv()
        front = []
        for m in range(6):
            packed = krecv[it, 1, m]
            front.append(jnp.where(low, klocal[1, 2 * m], half_turn(packed)))
            front.append(jnp.where(low, klocal[1, 2 * m + 1], packed))
        add_rebuilt(total, colour_mul(link(2), front, False), 2, -1.0)

        @pl.when(seg > 0)
        def _():
            to_s_up.wait_recv()

        @pl.when(seg < NY - 1)
        def _():
            to_s_down.wait_recv()

        for n in range(24):
            value = v(n)
            back, on = pltpu.roll(value, 1, 0), pltpu.roll(value, 7, 0)
            from_low = jnp.broadcast_to(srecv[it, 0, n : n + 1], (8, 128))
            from_high = jnp.broadcast_to(srecv[it, 1, n : n + 1], (8, 128))
            if n < 12:
                inner = jnp.where(sub < 4, back, on)
                moved = jnp.where(sub == 0, from_low, jnp.where(sub == 7, from_high, inner))
            else:
                inner = jnp.where(sub < 4, on, back)
                moved = jnp.where(sub == 4, from_low, jnp.where(sub == 3, from_high, inner))
            total[n] = total[n] - (1.0 / filter_radius) * moved

        to_t_up.wait_recv()
        add_rebuilt(total, [trecv[it, 0, n] for n in range(12)], 3, 1.0)
        to_t_down.wait_recv()
        front = [trecv[it, 1, n] for n in range(12)]
        add_rebuilt(total, colour_mul(link(3), front, False), 3, -1.0)

        gain = jnp.where(it == 0, 1.0, 2.0)
        for n in range(24):
            signed = pltpu.roll(total[n], 4, 0)
            centred = (filter_center / filter_radius) * v(n)
            inner = (signed if n < 12 else -signed) - centred
            field[it + 2, n] = gain * inner - field[it, n]
        return carry

    lax.fori_loop(0, DEGREE, step, 0)

    for n in range(24):
        ostage[pl.ds(n, 8, stride=24), :] = field[DEGREE + 1, n]

    def back_copy(n):
        return pltpu.make_async_remote_copy(
            src_ref=block(ostage, n),
            dst_ref=block(o_in, x),
            send_sem=send2.at[n],
            recv_sem=recv2.at[x],
            device_id=(sources[n], t),
            device_id_type=MESH,
        )

    for hi in range(NHI):
        for n in range(4):

            @pl.when(jnp.logical_not(to_self & (slot == n)) & (lax.rem(sources[n], NHI) == hi))
            def _():
                back_copy(n).start()

        if hi == 0:
            for r in range(ROUNDS):
                for side in (KP, KM):
                    pl.semaphore_signal(phase.at[r], inc=1, device_id=near[side], device_id_type=MESH)
                pl.semaphore_wait(phase.at[r], 2)

        if hi < NHI - 1:
            for n in range(4):

                @pl.when(jnp.logical_not(to_self & (slot == n)) & (lax.rem(sources[n], NHI) == hi))
                def _():
                    back_copy(n).wait_send()

    @pl.when(to_self)
    def _():
        mine = pltpu.make_async_copy(block(ostage, slot), block(o_in, x), local.at[0])
        mine.start()
        mine.wait()

    for q in range(NX):

        @pl.when(jnp.logical_not(to_self & (x == q)))
        def _():
            pltpu.make_async_remote_copy(
                src_ref=block(ostage, 0),
                dst_ref=block(o_in, q),
                send_sem=send2.at[0],
                recv_sem=recv2.at[q],
                device_id=near[TP],
                device_id_type=MESH,
            ).wait_recv()

        for s in range(2):
            for b in range(3):
                row = pl.multiple_of(q * 48 + lax.rem(s + flip, 2) * 24 + b * 8, 8)
                out_ref[pl.ds((s * 24 + b * 8) * 4 + q, 8, stride=4), :] = o_in[pl.ds(row, 8), :]

    for q in range(NX):
        other = jnp.logical_not(to_self & (x == q))

        @pl.when(other)
        def _():
            out_copy(q).wait_send()

        @pl.when(other & gives_links)
        def _():
            link_copy(q).wait_send()

    def sent(it, carry):
        def left(side, source, target):
            pltpu.make_async_remote_copy(
                src_ref=source,
                dst_ref=target,
                send_sem=sendh.at[it, side],
                recv_sem=recvh.at[it, side],
                device_id=near[side],
                device_id_type=MESH,
            ).wait_send()

        left(TP, tsend.at[it, 0], trecv.at[it, 0])
        left(TM, tsend.at[it, 1], trecv.at[it, 1])
        left(KP, ksend.at[it, 0], krecv.at[it, 0])
        left(KM, ksend.at[it, 1], krecv.at[it, 1])

        @pl.when(seg < NY - 1)
        def _():
            left(SP, ssend.at[it, 0], srecv.at[it, 0])

        @pl.when(seg > 0)
        def _():
            left(SM, ssend.at[it, 1], srecv.at[it, 1])

        return carry

    lax.fori_loop(0, DEGREE, sent, 0)

    for n in range(4):

        @pl.when(jnp.logical_not(to_self & (slot == n)) & (lax.rem(sources[n], NHI) == NHI - 1))
        def _():
            back_copy(n).wait_send()


def solution(mesh):
    nlo = mesh.shape["space"] // (NX * NC)
    vmem = pl.BlockSpec(memory_space=pltpu.VMEM)

    def f32(*shape):
        return pltpu.VMEM(shape, jnp.float32)

    dma = pltpu.SemaphoreType.DMA

    def on_device(spinor, gauge_links):
        out = pl.pallas_call(
            functools.partial(kernel, nlo),
            out_shape=jax.ShapeDtypeStruct((192, 128), jnp.float32),
            in_specs=[pl.BlockSpec(memory_space=pl.ANY)] * 2,
            out_specs=vmem,
            scratch_shapes=[
                f32(192, 128),
                f32(288, 128),
                f32(192, 128),
                f32(192, 128),
                f32(192, 128),
                f32(48, 128),
                f32(72, 8, 128),
                f32(DEGREE + 2, 24, 8, 128),
                f32(DEGREE, 2, 12, 8, 128),
                f32(DEGREE, 2, 12, 8, 128),
                f32(DEGREE, 2, 6, 8, 128),
                f32(DEGREE, 2, 6, 8, 128),
                f32(2, 12, 8, 128),
                f32(DEGREE, 2, 24, 128),
                f32(DEGREE, 2, 24, 128),
                f32(192, 128),
                f32(192, 128),
                dma((4,)),
                dma((4,)),
                dma((4,)),
                dma((1,)),
                dma((DEGREE, 6)),
                dma((DEGREE, 6)),
                dma((4,)),
                dma((4,)),
                dma((4,)),
                pltpu.SemaphoreType.REGULAR((ROUNDS,)),
            ],
            compiler_params=pltpu.CompilerParams(
                collective_id=0, has_side_effects=True, vmem_limit_bytes=60 * 2**20
            ),
        )(spinor.reshape(192, 128), gauge_links.reshape(288, 128))
        return out.reshape(2, 24, 1, 512)

    return jax.shard_map(
        on_device,
        mesh=mesh,
        in_specs=(P("fifth", None, "space", None), P(None, None, "space", None)),
        out_specs=P("fifth", None, "space", None),
        check_vma=False,
    )
```

```python
import functools

import jax
import jax.numpy as jnp
from jax import lax
from jax.experimental import pallas as pl
from jax.experimental.pallas import tpu as pltpu
from jax.sharding import PartitionSpec as P

MESH = pl.DeviceIdType.MESH
wall_height = 1.8
quark_mass = 0.1
filter_center = 0.5
filter_radius = 8.0
DEGREE = 4
gamma_block = (((1, 1), (0, 1)), ((1, 2), (0, 0)), ((0, 1), (1, 3)), ((0, 0), (1, 0)))
gamma_adjoint = (((1, 3), (0, 3)), ((1, 0), (0, 2)), ((0, 3), (1, 1)), ((0, 0), (1, 0)))
NX, NY, NHI, NC = 4, 4, 4, 2
Z_OFFSET = 7
Z_SIGN = -1
TP, TM, KP, KM, SP, SM = range(6)


def unit_part(quarter, part):
    if part == 0:
        return ((1.0, 0), (-1.0, 1), (-1.0, 0), (1.0, 1))[quarter]
    return ((1.0, 1), (1.0, 0), (-1.0, 1), (-1.0, 0))[quarter]


def plus(value, sign, term):
    return value + term if sign > 0 else value - term


def comp(spin, colour, part):
    return (spin * 3 + colour) * 2 + part


def project(field, direction, parity):
    half = []
    for row in range(2):
        source, quarter = gamma_block[direction][row]
        for colour in range(3):
            for part in range(2):
                sign, other = unit_part(quarter, part)
                half.append(
                    plus(field(comp(row, colour, part)), parity * sign, field(comp(2 + source, colour, other)))
                )
    return half


def add_rebuilt(total, half, direction, parity):
    for row in range(2):
        source, quarter = gamma_adjoint[direction][row]
        for colour in range(3):
            for part in range(2):
                n = comp(row, colour, part)
                total[n] = total[n] + half[n]
                sign, other = unit_part(quarter, part)
                m = comp(2 + row, colour, part)
                total[m] = plus(total[m], parity * sign, half[comp(source, colour, other)])


def colour_mul(link, half, dagger):
    result = [None] * 12
    for row in range(3):
        for column in range(3):
            if dagger:
                u_re, u_im, sign = link(column, row, 0), link(column, row, 1), -1.0
            else:
                u_re, u_im, sign = link(row, column, 0), link(row, column, 1), 1.0
            for spin in range(2):
                h_re, h_im = half[comp(spin, column, 0)], half[comp(spin, column, 1)]
                re = plus(u_re * h_re, -sign, u_im * h_im)
                im = plus(u_re * h_im, sign, u_im * h_re)
                r, i = comp(spin, row, 0), comp(spin, row, 1)
                result[r] = re if column == 0 else result[r] + re
                result[i] = im if column == 0 else result[i] + im
    return result


def kernel(
    nlo,
    sp_hbm,
    g_hbm,
    out_ref,
    sp_ref,
    g_ref,
    stage,
    gstage,
    psi_in,
    g_in,
    links,
    field,
    tsend,
    trecv,
    ksend,
    krecv,
    klocal,
    ssend,
    srecv,
    ostage,
    o_in,
    send1,
    recv1,
    sendg,
    recvg,
    sendh,
    recvh,
    send2,
    recv2,
    local,
):
    nz = NHI * nlo
    nt = nz * NC
    f = lax.axis_index("fifth")
    p = lax.axis_index("space")
    y, zhi = lax.div(f, NHI), lax.rem(f, NHI)
    zlo, x, c = lax.div(p, NX * NC), lax.rem(lax.div(p, NC), NX), lax.rem(p, NC)
    z = zhi * nlo + zlo

    def device(dx, dy, dz, dc):
        return (dy * NHI + lax.div(dz, nlo), lax.rem(dz, nlo) * (NX * NC) + dx * NC + dc)

    def z_of(time):
        return lax.rem(Z_SIGN * lax.div(time, NC) + Z_OFFSET + nz, nz)

    z_to = z_of(p)
    upper = f >= 8
    folded = jnp.where(upper, 15 - f, f)
    y_to = lax.rem(NY - lax.div(folded, 2), NY)
    slot = jnp.where(upper, 2, 0) + lax.rem(folded, 2)
    flip = jnp.where(upper, 1, 0)
    ahead = lax.rem(z_to - zlo + nz, nz)
    gives_links = zhi == lax.rem(lax.div(ahead + nlo // 2, nlo), NHI)
    to_self = (y_to == y) & (z_to == z)
    t = lax.rem(Z_SIGN * (z - Z_OFFSET) + nz + nz, nz) * NC + c
    seg = lax.rem(NY - y, NY)
    sources = (2 * seg, 2 * seg + 1, 15 - 2 * seg, 14 - 2 * seg)
    ahead_me = lax.rem(z - lax.div(t, NX * NC) + nz, nz)
    link_hi = lax.rem(lax.div(ahead_me + nlo // 2, nlo), NHI)

    t_up, t_down = lax.rem(t + 1, nt), lax.rem(t + nt - 1, nt)
    near = {
        TP: device(x, y, z_of(t_up), lax.rem(t_up, NC)),
        TM: device(x, y, z_of(t_down), lax.rem(t_down, NC)),
        KP: device(lax.rem(x + 1, NX), y, z, c),
        KM: device(lax.rem(x + NX - 1, NX), y, z, c),
        SP: device(x, lax.rem(y + NY - 1, NY), z, c),
        SM: device(x, lax.rem(y + 1, NY), z, c),
    }

    barrier = pltpu.get_barrier_semaphore()

    def greet(device_id):
        pl.semaphore_signal(barrier, inc=1, device_id=device_id, device_id_type=MESH)

    for n in range(4):

        @pl.when(jnp.logical_not(to_self & (slot == n)))
        def _():
            greet((sources[n], t))

    for side in (TP, TM, KP, KM):
        greet(near[side])

    @pl.when(seg < NY - 1)
    def _():
        greet(near[SP])

    @pl.when(seg > 0)
    def _():
        greet(near[SM])

    for source, target, sem in ((sp_hbm, sp_ref, 2), (g_hbm, g_ref, 3)):
        pltpu.make_async_copy(source, target, local.at[sem]).start()
    pltpu.make_async_copy(sp_hbm, sp_ref, local.at[2]).wait()

    for q in range(NX):
        for s in range(2):
            for b in range(3):
                row = pl.multiple_of(q * 48 + lax.rem(s + flip, 2) * 24 + b * 8, 8)
                stage[pl.ds(row, 8), :] = sp_ref[pl.ds((s * 24 + b * 8) * 4 + q, 8, stride=4), :]

    count = 8 - jnp.where(to_self, 1, 0) + jnp.where(seg > 0, 1, 0) + jnp.where(seg < NY - 1, 1, 0)
    pl.semaphore_wait(barrier, count)

    def block(ref, n):
        start = n * 48
        return ref.at[pl.ds(start if isinstance(n, int) else pl.multiple_of(start, 8), 48), :]

    def out_copy(q):
        return pltpu.make_async_remote_copy(
            src_ref=block(stage, q),
            dst_ref=block(psi_in, slot),
            send_sem=send1.at[q],
            recv_sem=recv1.at[slot],
            device_id=device(q, y_to, z_to, c),
            device_id_type=MESH,
        )

    def link_copy(q):
        return pltpu.make_async_remote_copy(
            src_ref=block(gstage, q),
            dst_ref=g_in,
            send_sem=sendg.at[q],
            recv_sem=recvg.at[0],
            device_id=device(q, y_to, z_to, c),
            device_id_type=MESH,
        )

    for q in range(NX):
        other = jnp.logical_not(to_self & (x == q))

        @pl.when(other)
        def _():
            out_copy(q).start()

    pltpu.make_async_copy(g_hbm, g_ref, local.at[3]).wait()

    @pl.when(gives_links)
    def _():
        for q in range(NX):
            for mu in range(4):
                first = g_ref[pl.ds(mu * 72 + q, 8, stride=4), :]
                gstage[q * 48 + mu * 12 : q * 48 + mu * 12 + 8, :] = first
                last = g_ref[pl.ds(mu * 72 + 32 + q, 4, stride=4), :]
                gstage[q * 48 + mu * 12 + 8 : q * 48 + mu * 12 + 12, :] = last

    for q in range(NX):

        @pl.when(jnp.logical_not(to_self & (x == q)) & gives_links)
        def _():
            link_copy(q).start()

    @pl.when(to_self)
    def _():
        mine = pltpu.make_async_copy(block(stage, x), block(psi_in, slot), local.at[0])
        mine.start()
        mine.wait()

    @pl.when(to_self & gives_links)
    def _():
        mine = pltpu.make_async_copy(block(gstage, x), g_in, local.at[1])
        mine.start()
        mine.wait()

    for n in range(24):
        field[0, n] = jnp.zeros((8, 128), jnp.float32)

    @pl.when(jnp.logical_not(to_self & (zhi == link_hi)))
    def _():
        link_copy(0).wait_recv()

    for mu in range(4):
        scale = -0.5 / filter_radius
        if mu == 3:
            scale = scale * jnp.where(t == nt - 1, -1.0, 1.0)
        rows = [
            jnp.broadcast_to(g_in[mu * 12 + r : mu * 12 + r + 1, :], (8, 128)) for r in range(12)
        ]
        for r in range(12):
            links[mu * 18 + r] = rows[r] * scale
        for i in range(3):
            j, k = (i + 1) % 3, (i + 2) % 3
            a_re, a_im, b_re, b_im = rows[2 * j], rows[2 * j + 1], rows[6 + 2 * k], rows[7 + 2 * k]
            c_re, c_im, d_re, d_im = rows[2 * k], rows[2 * k + 1], rows[6 + 2 * j], rows[7 + 2 * j]
            re = (a_re * b_re - a_im * b_im) - (c_re * d_re - c_im * d_im)
            im = (c_re * d_im + c_im * d_re) - (a_re * b_im + a_im * b_re)
            links[mu * 18 + 12 + 2 * i] = re * scale
            links[mu * 18 + 13 + 2 * i] = im * scale

    for n in range(4):

        @pl.when(jnp.logical_not(to_self & (slot == n)))
        def _():
            pltpu.make_async_remote_copy(
                src_ref=block(stage, 0),
                dst_ref=block(psi_in, n),
                send_sem=send1.at[0],
                recv_sem=recv1.at[n],
                device_id=near[TP],
                device_id_type=MESH,
            ).wait_recv()

    for n in range(24):
        field[1, n] = psi_in[pl.ds(n, 8, stride=24), :]

    lane = lax.broadcasted_iota(jnp.int32, (8, 128), 1)
    sub = lax.broadcasted_iota(jnp.int32, (8, 128), 0)
    low = lane < 64

    def shift(value, direction, forward):
        stride = 8**direction
        position = lax.rem(lax.div(lane, stride), 8)
        inside, outside = (128 - stride, 7 * stride) if forward else (stride, 128 - 7 * stride)
        edge = position == (7 if forward else 0)
        return jnp.where(edge, pltpu.roll(value, outside, 1), pltpu.roll(value, inside, 1))

    def half_turn(value):
        return pltpu.roll(value, 64, 1)

    def step(it, carry):
        def v(n):
            return field[it + 1, n]

        def link(mu):
            return lambda row, column, part: links[mu * 18 + (row * 3 + column) * 2 + part]

        def halo(side, source, target):
            return pltpu.make_async_remote_copy(
                src_ref=source,
                dst_ref=target,
                send_sem=sendh.at[it, side],
                recv_sem=recvh.at[it, side],
                device_id=near[side],
                device_id_type=MESH,
            )

        to_t_up = halo(TP, tsend.at[it, 0], trecv.at[it, 0])
        to_t_down = halo(TM, tsend.at[it, 1], trecv.at[it, 1])
        to_k_up = halo(KP, ksend.at[it, 0], krecv.at[it, 0])
        to_k_down = halo(KM, ksend.at[it, 1], krecv.at[it, 1])
        to_s_up = halo(SP, ssend.at[it, 0], srecv.at[it, 0])
        to_s_down = halo(SM, ssend.at[it, 1], srecv.at[it, 1])

        behind = colour_mul(link(3), project(v, 3, 1.0), True)
        for n in range(12):
            tsend[it, 0, n] = behind[n]
        to_t_up.start()
        front = project(v, 3, -1.0)
        for n in range(12):
            tsend[it, 1, n] = front[n]
        to_t_down.start()

        behind = colour_mul(link(2), project(v, 2, 1.0), True)
        for m in range(6):
            a, b = behind[2 * m], behind[2 * m + 1]
            ra, rb = half_turn(a), half_turn(b)
            ksend[it, 0, m] = jnp.where(low, ra, b)
            klocal[0, 2 * m] = ra
            klocal[0, 2 * m + 1] = rb
        to_k_up.start()
        front = project(v, 2, -1.0)
        for m in range(6):
            a, b = front[2 * m], front[2 * m + 1]
            ra, rb = half_turn(a), half_turn(b)
            ksend[it, 1, m] = jnp.where(low, a, rb)
            klocal[1, 2 * m] = ra
            klocal[1, 2 * m + 1] = rb
        to_k_down.start()

        for n in range(24):
            value = v(n)
            up, down = (3, 4) if n < 12 else (7, 0)
            ssend[it, 0, n : n + 1] = value[up : up + 1]
            ssend[it, 1, n : n + 1] = value[down : down + 1]

        @pl.when(seg < NY - 1)
        def _():
            to_s_up.start()

        @pl.when(seg > 0)
        def _():
            to_s_down.start()

        @pl.when(seg == NY - 1)
        def _():
            srecv[it, 1] = ssend[it, 0]

        @pl.when(seg == 0)
        def _():
            srecv[it, 0] = ssend[it, 1] * -quark_mass

        total = [((5.0 - wall_height) / filter_radius) * v(n) for n in range(24)]
        for direction in range(2):
            front = [shift(value, direction, True) for value in project(v, direction, -1.0)]
            add_rebuilt(total, colour_mul(link(direction), front, False), direction, -1.0)
            behind = colour_mul(link(direction), project(v, direction, 1.0), True)
            add_rebuilt(total, [shift(value, direction, False) for value in behind], direction, 1.0)

        to_k_up.wait_recv()
        behind = []
        for m in range(6):
            packed = krecv[it, 0, m]
            behind.append(jnp.where(low, packed, klocal[0, 2 * m]))
            behind.append(jnp.where(low, half_turn(packed), klocal[0, 2 * m + 1]))
        add_rebuilt(total, behind, 2, 1.0)
        to_k_down.wait_recv()
        front = []
        for m in range(6):
            packed = krecv[it, 1, m]
            front.append(jnp.where(low, klocal[1, 2 * m], half_turn(packed)))
            front.append(jnp.where(low, klocal[1, 2 * m + 1], packed))
        add_rebuilt(total, colour_mul(link(2), front, False), 2, -1.0)

        @pl.when(seg > 0)
        def _():
            to_s_up.wait_recv()

        @pl.when(seg < NY - 1)
        def _():
            to_s_down.wait_recv()

        for n in range(24):
            value = v(n)
            back, on = pltpu.roll(value, 1, 0), pltpu.roll(value, 7, 0)
            from_low = jnp.broadcast_to(srecv[it, 0, n : n + 1], (8, 128))
            from_high = jnp.broadcast_to(srecv[it, 1, n : n + 1], (8, 128))
            if n < 12:
                inner = jnp.where(sub < 4, back, on)
                moved = jnp.where(sub == 0, from_low, jnp.where(sub == 7, from_high, inner))
            else:
                inner = jnp.where(sub < 4, on, back)
                moved = jnp.where(sub == 4, from_low, jnp.where(sub == 3, from_high, inner))
            total[n] = total[n] - (1.0 / filter_radius) * moved

        to_t_up.wait_recv()
        add_rebuilt(total, [trecv[it, 0, n] for n in range(12)], 3, 1.0)
        to_t_down.wait_recv()
        front = [trecv[it, 1, n] for n in range(12)]
        add_rebuilt(total, colour_mul(link(3), front, False), 3, -1.0)

        gain = jnp.where(it == 0, 1.0, 2.0)
        for n in range(24):
            signed = pltpu.roll(total[n], 4, 0)
            centred = (filter_center / filter_radius) * v(n)
            inner = (signed if n < 12 else -signed) - centred
            field[it + 2, n] = gain * inner - field[it, n]
        return carry

    lax.fori_loop(0, DEGREE, step, 0)

    for n in range(24):
        ostage[pl.ds(n, 8, stride=24), :] = field[DEGREE + 1, n]

    def back_copy(n):
        return pltpu.make_async_remote_copy(
            src_ref=block(ostage, n),
            dst_ref=block(o_in, x),
            send_sem=send2.at[n],
            recv_sem=recv2.at[x],
            device_id=(sources[n], t),
            device_id_type=MESH,
        )

    for hi in range(NHI):
        for n in range(4):

            @pl.when(jnp.logical_not(to_self & (slot == n)) & (lax.rem(sources[n], NHI) == hi))
            def _():
                back_copy(n).start()

        if hi < NHI - 1:
            for n in range(4):

                @pl.when(jnp.logical_not(to_self & (slot == n)) & (lax.rem(sources[n], NHI) == hi))
                def _():
                    back_copy(n).wait_send()

    @pl.when(to_self)
    def _():
        mine = pltpu.make_async_copy(block(ostage, slot), block(o_in, x), local.at[0])
        mine.start()
        mine.wait()

    for q in range(NX):

        @pl.when(jnp.logical_not(to_self & (x == q)))
        def _():
            pltpu.make_async_remote_copy(
                src_ref=block(ostage, 0),
                dst_ref=block(o_in, q),
                send_sem=send2.at[0],
                recv_sem=recv2.at[q],
                device_id=near[TP],
                device_id_type=MESH,
            ).wait_recv()

        for s in range(2):
            for b in range(3):
                row = pl.multiple_of(q * 48 + lax.rem(s + flip, 2) * 24 + b * 8, 8)
                out_ref[pl.ds((s * 24 + b * 8) * 4 + q, 8, stride=4), :] = o_in[pl.ds(row, 8), :]

    for q in range(NX):
        other = jnp.logical_not(to_self & (x == q))

        @pl.when(other)
        def _():
            out_copy(q).wait_send()

        @pl.when(other & gives_links)
        def _():
            link_copy(q).wait_send()

    def sent(it, carry):
        def left(side, source, target):
            pltpu.make_async_remote_copy(
                src_ref=source,
                dst_ref=target,
                send_sem=sendh.at[it, side],
                recv_sem=recvh.at[it, side],
                device_id=near[side],
                device_id_type=MESH,
            ).wait_send()

        left(TP, tsend.at[it, 0], trecv.at[it, 0])
        left(TM, tsend.at[it, 1], trecv.at[it, 1])
        left(KP, ksend.at[it, 0], krecv.at[it, 0])
        left(KM, ksend.at[it, 1], krecv.at[it, 1])

        @pl.when(seg < NY - 1)
        def _():
            left(SP, ssend.at[it, 0], srecv.at[it, 0])

        @pl.when(seg > 0)
        def _():
            left(SM, ssend.at[it, 1], srecv.at[it, 1])

        return carry

    lax.fori_loop(0, DEGREE, sent, 0)

    for n in range(4):

        @pl.when(jnp.logical_not(to_self & (slot == n)) & (lax.rem(sources[n], NHI) == NHI - 1))
        def _():
            back_copy(n).wait_send()


def solution(mesh):
    nlo = mesh.shape["space"] // (NX * NC)
    vmem = pl.BlockSpec(memory_space=pltpu.VMEM)

    def f32(*shape):
        return pltpu.VMEM(shape, jnp.float32)

    dma = pltpu.SemaphoreType.DMA

    def on_device(spinor, gauge_links):
        out = pl.pallas_call(
            functools.partial(kernel, nlo),
            out_shape=jax.ShapeDtypeStruct((192, 128), jnp.float32),
            in_specs=[pl.BlockSpec(memory_space=pltpu.HBM)] * 2,
            out_specs=vmem,
            scratch_shapes=[
                f32(192, 128),
                f32(288, 128),
                f32(192, 128),
                f32(192, 128),
                f32(192, 128),
                f32(48, 128),
                f32(72, 8, 128),
                f32(DEGREE + 2, 24, 8, 128),
                f32(DEGREE, 2, 12, 8, 128),
                f32(DEGREE, 2, 12, 8, 128),
                f32(DEGREE, 2, 6, 8, 128),
                f32(DEGREE, 2, 6, 8, 128),
                f32(2, 12, 8, 128),
                f32(DEGREE, 2, 24, 128),
                f32(DEGREE, 2, 24, 128),
                f32(192, 128),
                f32(192, 128),
                dma((4,)),
                dma((4,)),
                dma((4,)),
                dma((1,)),
                dma((DEGREE, 6)),
                dma((DEGREE, 6)),
                dma((4,)),
                dma((4,)),
                dma((4,)),
            ],
            compiler_params=pltpu.CompilerParams(
                collective_id=0, has_side_effects=True, vmem_limit_bytes=55104 * 1024
            ),
        )(spinor.reshape(192, 128), gauge_links.reshape(288, 128))
        return out.reshape(2, 24, 1, 512)

    return jax.shard_map(
        on_device,
        mesh=mesh,
        in_specs=(P("fifth", None, "space", None), P(None, None, "space", None)),
        out_specs=P("fifth", None, "space", None),
        check_vma=False,
    )
```

```python
import functools

import jax
import jax.numpy as jnp
from jax import lax
from jax.experimental import pallas as pl
from jax.experimental.pallas import tpu as pltpu
from jax.sharding import PartitionSpec as P

MESH = pl.DeviceIdType.MESH
wall_height = 1.8
quark_mass = 0.1
filter_center = 0.5
filter_radius = 8.0
DEGREE = 4
gamma_block = (((1, 1), (0, 1)), ((1, 2), (0, 0)), ((0, 1), (1, 3)), ((0, 0), (1, 0)))
gamma_adjoint = (((1, 3), (0, 3)), ((1, 0), (0, 2)), ((0, 3), (1, 1)), ((0, 0), (1, 0)))
NX, NY, NHI, NC = 4, 4, 4, 2
Z_OFFSET = 5
Z_SIGN = -1
TP, TM, KP, KM, SP, SM = range(6)


def unit_part(quarter, part):
    if part == 0:
        return ((1.0, 0), (-1.0, 1), (-1.0, 0), (1.0, 1))[quarter]
    return ((1.0, 1), (1.0, 0), (-1.0, 1), (-1.0, 0))[quarter]


def plus(value, sign, term):
    return value + term if sign > 0 else value - term


def comp(spin, colour, part):
    return (spin * 3 + colour) * 2 + part


def project(field, direction, parity):
    half = []
    for row in range(2):
        source, quarter = gamma_block[direction][row]
        for colour in range(3):
            for part in range(2):
                sign, other = unit_part(quarter, part)
                half.append(
                    plus(field(comp(row, colour, part)), parity * sign, field(comp(2 + source, colour, other)))
                )
    return half


def add_rebuilt(total, half, direction, parity):
    for row in range(2):
        source, quarter = gamma_adjoint[direction][row]
        for colour in range(3):
            for part in range(2):
                n = comp(row, colour, part)
                total[n] = total[n] + half[n]
                sign, other = unit_part(quarter, part)
                m = comp(2 + row, colour, part)
                total[m] = plus(total[m], parity * sign, half[comp(source, colour, other)])


def colour_mul(link, half, dagger):
    result = [None] * 12
    for row in range(3):
        for column in range(3):
            if dagger:
                u_re, u_im, sign = link(column, row, 0), link(column, row, 1), -1.0
            else:
                u_re, u_im, sign = link(row, column, 0), link(row, column, 1), 1.0
            for spin in range(2):
                h_re, h_im = half[comp(spin, column, 0)], half[comp(spin, column, 1)]
                re = plus(u_re * h_re, -sign, u_im * h_im)
                im = plus(u_re * h_im, sign, u_im * h_re)
                r, i = comp(spin, row, 0), comp(spin, row, 1)
                result[r] = re if column == 0 else result[r] + re
                result[i] = im if column == 0 else result[i] + im
    return result


def kernel(
    nlo,
    sp_hbm,
    g_hbm,
    out_ref,
    sp_ref,
    g_ref,
    stage,
    gstage,
    psi_in,
    g_in,
    links,
    field,
    tsend,
    trecv,
    ksend,
    krecv,
    klocal,
    ssend,
    srecv,
    ostage,
    o_in,
    send1,
    recv1,
    sendg,
    recvg,
    sendh,
    recvh,
    send2,
    recv2,
    local,
):
    nz = NHI * nlo
    nt = nz * NC
    f = lax.axis_index("fifth")
    p = lax.axis_index("space")
    y, zhi = lax.div(f, NHI), lax.rem(f, NHI)
    zlo, x, c = lax.div(p, NX * NC), lax.rem(lax.div(p, NC), NX), lax.rem(p, NC)
    z = zhi * nlo + zlo

    def device(dx, dy, dz, dc):
        return (dy * NHI + lax.div(dz, nlo), lax.rem(dz, nlo) * (NX * NC) + dx * NC + dc)

    def z_of(time):
        return lax.rem(Z_SIGN * lax.div(time, NC) + Z_OFFSET + nz, nz)

    z_to = z_of(p)
    upper = f >= 8
    folded = jnp.where(upper, 15 - f, f)
    y_to = lax.rem(NY - lax.div(folded, 2), NY)
    slot = jnp.where(upper, 2, 0) + lax.rem(folded, 2)
    flip = jnp.where(upper, 1, 0)
    ahead = lax.rem(z_to - zlo + nz, nz)
    gives_links = zhi == lax.rem(lax.div(ahead + nlo // 2, nlo), NHI)
    to_self = (y_to == y) & (z_to == z)
    t = lax.rem(Z_SIGN * (z - Z_OFFSET) + nz + nz, nz) * NC + c
    seg = lax.rem(NY - y, NY)
    sources = (2 * seg, 2 * seg + 1, 15 - 2 * seg, 14 - 2 * seg)
    ahead_me = lax.rem(z - lax.div(t, NX * NC) + nz, nz)
    link_hi = lax.rem(lax.div(ahead_me + nlo // 2, nlo), NHI)

    t_up, t_down = lax.rem(t + 1, nt), lax.rem(t + nt - 1, nt)
    near = {
        TP: device(x, y, z_of(t_up), lax.rem(t_up, NC)),
        TM: device(x, y, z_of(t_down), lax.rem(t_down, NC)),
        KP: device(lax.rem(x + 1, NX), y, z, c),
        KM: device(lax.rem(x + NX - 1, NX), y, z, c),
        SP: device(x, lax.rem(y + NY - 1, NY), z, c),
        SM: device(x, lax.rem(y + 1, NY), z, c),
    }

    barrier = pltpu.get_barrier_semaphore()

    def greet(device_id):
        pl.semaphore_signal(barrier, inc=1, device_id=device_id, device_id_type=MESH)

    for n in range(4):

        @pl.when(jnp.logical_not(to_self & (slot == n)))
        def _():
            greet((sources[n], t))

    for side in (TP, TM, KP, KM):
        greet(near[side])

    @pl.when(seg < NY - 1)
    def _():
        greet(near[SP])

    @pl.when(seg > 0)
    def _():
        greet(near[SM])

    for source, target, sem in ((sp_hbm, sp_ref, 2), (g_hbm, g_ref, 3)):
        pltpu.make_async_copy(source, target, local.at[sem]).start()
    pltpu.make_async_copy(sp_hbm, sp_ref, local.at[2]).wait()
    pltpu.make_async_copy(g_hbm, g_ref, local.at[3]).wait()

    for q in range(NX):
        for s in range(2):
            for b in range(3):
                row = pl.multiple_of(q * 48 + lax.rem(s + flip, 2) * 24 + b * 8, 8)
                stage[pl.ds(row, 8), :] = sp_ref[pl.ds((s * 24 + b * 8) * 4 + q, 8, stride=4), :]
        for mu in range(4):
            first = g_ref[pl.ds(mu * 72 + q, 8, stride=4), :]
            gstage[q * 48 + mu * 12 : q * 48 + mu * 12 + 8, :] = first
            last = g_ref[pl.ds(mu * 72 + 32 + q, 4, stride=4), :]
            gstage[q * 48 + mu * 12 + 8 : q * 48 + mu * 12 + 12, :] = last

    count = 8 - jnp.where(to_self, 1, 0) + jnp.where(seg > 0, 1, 0) + jnp.where(seg < NY - 1, 1, 0)
    pl.semaphore_wait(barrier, count)

    def block(ref, n):
        start = n * 48
        return ref.at[pl.ds(start if isinstance(n, int) else pl.multiple_of(start, 8), 48), :]

    def out_copy(q):
        return pltpu.make_async_remote_copy(
            src_ref=block(stage, q),
            dst_ref=block(psi_in, slot),
            send_sem=send1.at[q],
            recv_sem=recv1.at[slot],
            device_id=device(q, y_to, z_to, c),
            device_id_type=MESH,
        )

    def link_copy(q):
        return pltpu.make_async_remote_copy(
            src_ref=block(gstage, q),
            dst_ref=g_in,
            send_sem=sendg.at[q],
            recv_sem=recvg.at[0],
            device_id=device(q, y_to, z_to, c),
            device_id_type=MESH,
        )

    for q in range(NX):
        other = jnp.logical_not(to_self & (x == q))

        @pl.when(other)
        def _():
            out_copy(q).start()

        @pl.when(other & gives_links)
        def _():
            link_copy(q).start()

    @pl.when(to_self)
    def _():
        mine = pltpu.make_async_copy(block(stage, x), block(psi_in, slot), local.at[0])
        mine.start()
        mine.wait()

    @pl.when(to_self & gives_links)
    def _():
        mine = pltpu.make_async_copy(block(gstage, x), g_in, local.at[1])
        mine.start()
        mine.wait()

    for n in range(24):
        field[0, n] = jnp.zeros((8, 128), jnp.float32)

    @pl.when(jnp.logical_not(to_self & (zhi == link_hi)))
    def _():
        link_copy(0).wait_recv()

    for mu in range(4):
        scale = -0.5 / filter_radius
        if mu == 3:
            scale = scale * jnp.where(t == nt - 1, -1.0, 1.0)
        rows = [
            jnp.broadcast_to(g_in[mu * 12 + r : mu * 12 + r + 1, :], (8, 128)) for r in range(12)
        ]
        for r in range(12):
            links[mu * 18 + r] = rows[r] * scale
        for i in range(3):
            j, k = (i + 1) % 3, (i + 2) % 3
            a_re, a_im, b_re, b_im = rows[2 * j], rows[2 * j + 1], rows[6 + 2 * k], rows[7 + 2 * k]
            c_re, c_im, d_re, d_im = rows[2 * k], rows[2 * k + 1], rows[6 + 2 * j], rows[7 + 2 * j]
            re = (a_re * b_re - a_im * b_im) - (c_re * d_re - c_im * d_im)
            im = (c_re * d_im + c_im * d_re) - (a_re * b_im + a_im * b_re)
            links[mu * 18 + 12 + 2 * i] = re * scale
            links[mu * 18 + 13 + 2 * i] = im * scale

    for n in range(4):

        @pl.when(jnp.logical_not(to_self & (slot == n)))
        def _():
            pltpu.make_async_remote_copy(
                src_ref=block(stage, 0),
                dst_ref=block(psi_in, n),
                send_sem=send1.at[0],
                recv_sem=recv1.at[n],
                device_id=near[TP],
                device_id_type=MESH,
            ).wait_recv()

    for n in range(24):
        field[1, n] = psi_in[pl.ds(n, 8, stride=24), :]

    lane = lax.broadcasted_iota(jnp.int32, (8, 128), 1)
    sub = lax.broadcasted_iota(jnp.int32, (8, 128), 0)
    low = lane < 64

    def shift(value, direction, forward):
        stride = 8**direction
        position = lax.rem(lax.div(lane, stride), 8)
        inside, outside = (128 - stride, 7 * stride) if forward else (stride, 128 - 7 * stride)
        edge = position == (7 if forward else 0)
        return jnp.where(edge, pltpu.roll(value, outside, 1), pltpu.roll(value, inside, 1))

    def half_turn(value):
        return pltpu.roll(value, 64, 1)

    def step(it, carry):
        def v(n):
            return field[it + 1, n]

        def link(mu):
            return lambda row, column, part: links[mu * 18 + (row * 3 + column) * 2 + part]

        def halo(side, source, target):
            return pltpu.make_async_remote_copy(
                src_ref=source,
                dst_ref=target,
                send_sem=sendh.at[it, side],
                recv_sem=recvh.at[it, side],
                device_id=near[side],
                device_id_type=MESH,
            )

        to_t_up = halo(TP, tsend.at[it, 0], trecv.at[it, 0])
        to_t_down = halo(TM, tsend.at[it, 1], trecv.at[it, 1])
        to_k_up = halo(KP, ksend.at[it, 0], krecv.at[it, 0])
        to_k_down = halo(KM, ksend.at[it, 1], krecv.at[it, 1])
        to_s_up = halo(SP, ssend.at[it, 0], srecv.at[it, 0])
        to_s_down = halo(SM, ssend.at[it, 1], srecv.at[it, 1])

        behind = colour_mul(link(3), project(v, 3, 1.0), True)
        for n in range(12):
            tsend[it, 0, n] = behind[n]
        to_t_up.start()
        front = project(v, 3, -1.0)
        for n in range(12):
            tsend[it, 1, n] = front[n]
        to_t_down.start()

        behind = colour_mul(link(2), project(v, 2, 1.0), True)
        for m in range(6):
            a, b = behind[2 * m], behind[2 * m + 1]
            ra, rb = half_turn(a), half_turn(b)
            ksend[it, 0, m] = jnp.where(low, ra, b)
            klocal[0, 2 * m] = ra
            klocal[0, 2 * m + 1] = rb
        to_k_up.start()
        front = project(v, 2, -1.0)
        for m in range(6):
            a, b = front[2 * m], front[2 * m + 1]
            ra, rb = half_turn(a), half_turn(b)
            ksend[it, 1, m] = jnp.where(low, a, rb)
            klocal[1, 2 * m] = ra
            klocal[1, 2 * m + 1] = rb
        to_k_down.start()

        for n in range(24):
            value = v(n)
            up, down = (3, 4) if n < 12 else (7, 0)
            ssend[it, 0, n : n + 1] = value[up : up + 1]
            ssend[it, 1, n : n + 1] = value[down : down + 1]

        @pl.when(seg < NY - 1)
        def _():
            to_s_up.start()

        @pl.when(seg > 0)
        def _():
            to_s_down.start()

        @pl.when(seg == NY - 1)
        def _():
            srecv[it, 1] = ssend[it, 0]

        @pl.when(seg == 0)
        def _():
            srecv[it, 0] = ssend[it, 1] * -quark_mass

        total = [((5.0 - wall_height) / filter_radius) * v(n) for n in range(24)]
        for direction in range(2):
            front = [shift(value, direction, True) for value in project(v, direction, -1.0)]
            add_rebuilt(total, colour_mul(link(direction), front, False), direction, -1.0)
            behind = colour_mul(link(direction), project(v, direction, 1.0), True)
            add_rebuilt(total, [shift(value, direction, False) for value in behind], direction, 1.0)

        to_k_up.wait_recv()
        behind = []
        for m in range(6):
            packed = krecv[it, 0, m]
            behind.append(jnp.where(low, packed, klocal[0, 2 * m]))
            behind.append(jnp.where(low, half_turn(packed), klocal[0, 2 * m + 1]))
        add_rebuilt(total, behind, 2, 1.0)
        to_k_down.wait_recv()
        front = []
        for m in range(6):
            packed = krecv[it, 1, m]
            front.append(jnp.where(low, klocal[1, 2 * m], half_turn(packed)))
            front.append(jnp.where(low, klocal[1, 2 * m + 1], packed))
        add_rebuilt(total, colour_mul(link(2), front, False), 2, -1.0)

        @pl.when(seg > 0)
        def _():
            to_s_up.wait_recv()

        @pl.when(seg < NY - 1)
        def _():
            to_s_down.wait_recv()

        for n in range(24):
            value = v(n)
            back, on = pltpu.roll(value, 1, 0), pltpu.roll(value, 7, 0)
            from_low = jnp.broadcast_to(srecv[it, 0, n : n + 1], (8, 128))
            from_high = jnp.broadcast_to(srecv[it, 1, n : n + 1], (8, 128))
            if n < 12:
                inner = jnp.where(sub < 4, back, on)
                moved = jnp.where(sub == 0, from_low, jnp.where(sub == 7, from_high, inner))
            else:
                inner = jnp.where(sub < 4, on, back)
                moved = jnp.where(sub == 4, from_low, jnp.where(sub == 3, from_high, inner))
            total[n] = total[n] - (1.0 / filter_radius) * moved

        to_t_up.wait_recv()
        add_rebuilt(total, [trecv[it, 0, n] for n in range(12)], 3, 1.0)
        to_t_down.wait_recv()
        front = [trecv[it, 1, n] for n in range(12)]
        add_rebuilt(total, colour_mul(link(3), front, False), 3, -1.0)

        gain = jnp.where(it == 0, 1.0, 2.0)
        for n in range(24):
            signed = pltpu.roll(total[n], 4, 0)
            centred = (filter_center / filter_radius) * v(n)
            inner = (signed if n < 12 else -signed) - centred
            field[it + 2, n] = gain * inner - field[it, n]
        return carry

    lax.fori_loop(0, DEGREE, step, 0)

    for n in range(24):
        ostage[pl.ds(n, 8, stride=24), :] = field[DEGREE + 1, n]

    def back_copy(n):
        return pltpu.make_async_remote_copy(
            src_ref=block(ostage, n),
            dst_ref=block(o_in, x),
            send_sem=send2.at[n],
            recv_sem=recv2.at[x],
            device_id=(sources[n], t),
            device_id_type=MESH,
        )

    for hi in range(NHI):
        for n in range(4):

            @pl.when(jnp.logical_not(to_self & (slot == n)) & (lax.rem(sources[n], NHI) == hi))
            def _():
                back_copy(n).start()

        if hi < NHI - 1:
            for n in range(4):

                @pl.when(jnp.logical_not(to_self & (slot == n)) & (lax.rem(sources[n], NHI) == hi))
                def _():
                    back_copy(n).wait_send()

    @pl.when(to_self)
    def _():
        mine = pltpu.make_async_copy(block(ostage, slot), block(o_in, x), local.at[0])
        mine.start()
        mine.wait()

    for q in range(NX):

        @pl.when(jnp.logical_not(to_self & (x == q)))
        def _():
            pltpu.make_async_remote_copy(
                src_ref=block(ostage, 0),
                dst_ref=block(o_in, q),
                send_sem=send2.at[0],
                recv_sem=recv2.at[q],
                device_id=near[TP],
                device_id_type=MESH,
            ).wait_recv()

        for s in range(2):
            for b in range(3):
                row = pl.multiple_of(q * 48 + lax.rem(s + flip, 2) * 24 + b * 8, 8)
                out_ref[pl.ds((s * 24 + b * 8) * 4 + q, 8, stride=4), :] = o_in[pl.ds(row, 8), :]

    for q in range(NX):
        other = jnp.logical_not(to_self & (x == q))

        @pl.when(other)
        def _():
            out_copy(q).wait_send()

        @pl.when(other & gives_links)
        def _():
            link_copy(q).wait_send()

    def sent(it, carry):
        def left(side, source, target):
            pltpu.make_async_remote_copy(
                src_ref=source,
                dst_ref=target,
                send_sem=sendh.at[it, side],
                recv_sem=recvh.at[it, side],
                device_id=near[side],
                device_id_type=MESH,
            ).wait_send()

        left(TP, tsend.at[it, 0], trecv.at[it, 0])
        left(TM, tsend.at[it, 1], trecv.at[it, 1])
        left(KP, ksend.at[it, 0], krecv.at[it, 0])
        left(KM, ksend.at[it, 1], krecv.at[it, 1])

        @pl.when(seg < NY - 1)
        def _():
            left(SP, ssend.at[it, 0], srecv.at[it, 0])

        @pl.when(seg > 0)
        def _():
            left(SM, ssend.at[it, 1], srecv.at[it, 1])

        return carry

    lax.fori_loop(0, DEGREE, sent, 0)

    for n in range(4):

        @pl.when(jnp.logical_not(to_self & (slot == n)) & (lax.rem(sources[n], NHI) == NHI - 1))
        def _():
            back_copy(n).wait_send()


def solution(mesh):
    nlo = mesh.shape["space"] // (NX * NC)
    vmem = pl.BlockSpec(memory_space=pltpu.VMEM)

    def f32(*shape):
        return pltpu.VMEM(shape, jnp.float32)

    dma = pltpu.SemaphoreType.DMA

    def on_device(spinor, gauge_links):
        out = pl.pallas_call(
            functools.partial(kernel, nlo),
            out_shape=jax.ShapeDtypeStruct((192, 128), jnp.float32),
            in_specs=[pl.BlockSpec(memory_space=pltpu.HBM)] * 2,
            out_specs=vmem,
            scratch_shapes=[
                f32(192, 128),
                f32(288, 128),
                f32(192, 128),
                f32(192, 128),
                f32(192, 128),
                f32(48, 128),
                f32(72, 8, 128),
                f32(DEGREE + 2, 24, 8, 128),
                f32(DEGREE, 2, 12, 8, 128),
                f32(DEGREE, 2, 12, 8, 128),
                f32(DEGREE, 2, 6, 8, 128),
                f32(DEGREE, 2, 6, 8, 128),
                f32(2, 12, 8, 128),
                f32(DEGREE, 2, 24, 128),
                f32(DEGREE, 2, 24, 128),
                f32(192, 128),
                f32(192, 128),
                dma((4,)),
                dma((4,)),
                dma((4,)),
                dma((1,)),
                dma((DEGREE, 6)),
                dma((DEGREE, 6)),
                dma((4,)),
                dma((4,)),
                dma((4,)),
            ],
            compiler_params=pltpu.CompilerParams(
                collective_id=0, has_side_effects=True, vmem_limit_bytes=55104 * 1024
            ),
        )(spinor.reshape(192, 128), gauge_links.reshape(288, 128))
        return out.reshape(2, 24, 1, 512)

    return jax.shard_map(
        on_device,
        mesh=mesh,
        in_specs=(P("fifth", None, "space", None), P(None, None, "space", None)),
        out_specs=P("fifth", None, "space", None),
        check_vma=False,
    )
```

```python
import functools

import jax
import jax.numpy as jnp
from jax import lax
from jax.experimental import pallas as pl
from jax.experimental.pallas import tpu as pltpu
from jax.sharding import PartitionSpec as P

MESH = pl.DeviceIdType.MESH
wall_height = 1.8
quark_mass = 0.1
filter_center = 0.5
filter_radius = 8.0
DEGREE = 4
gamma_block = (((1, 1), (0, 1)), ((1, 2), (0, 0)), ((0, 1), (1, 3)), ((0, 0), (1, 0)))
gamma_adjoint = (((1, 3), (0, 3)), ((1, 0), (0, 2)), ((0, 3), (1, 1)), ((0, 0), (1, 0)))
NX, NY, NHI, NC = 4, 4, 4, 2
Z_OFFSET = 5
Z_SIGN = -1
TP, TM, KP, KM, SP, SM = range(6)


def unit_part(quarter, part):
    if part == 0:
        return ((1.0, 0), (-1.0, 1), (-1.0, 0), (1.0, 1))[quarter]
    return ((1.0, 1), (1.0, 0), (-1.0, 1), (-1.0, 0))[quarter]


def plus(value, sign, term):
    return value + term if sign > 0 else value - term


def comp(spin, colour, part):
    return (spin * 3 + colour) * 2 + part


def project(field, direction, parity):
    half = []
    for row in range(2):
        source, quarter = gamma_block[direction][row]
        for colour in range(3):
            for part in range(2):
                sign, other = unit_part(quarter, part)
                half.append(
                    plus(field(comp(row, colour, part)), parity * sign, field(comp(2 + source, colour, other)))
                )
    return half


def add_rebuilt(total, half, direction, parity):
    for row in range(2):
        source, quarter = gamma_adjoint[direction][row]
        for colour in range(3):
            for part in range(2):
                n = comp(row, colour, part)
                total[n] = total[n] + half[n]
                sign, other = unit_part(quarter, part)
                m = comp(2 + row, colour, part)
                total[m] = plus(total[m], parity * sign, half[comp(source, colour, other)])


def colour_mul(link, half, dagger):
    result = [None] * 12
    for row in range(3):
        for column in range(3):
            if dagger:
                u_re, u_im, sign = link(column, row, 0), link(column, row, 1), -1.0
            else:
                u_re, u_im, sign = link(row, column, 0), link(row, column, 1), 1.0
            for spin in range(2):
                h_re, h_im = half[comp(spin, column, 0)], half[comp(spin, column, 1)]
                re = plus(u_re * h_re, -sign, u_im * h_im)
                im = plus(u_re * h_im, sign, u_im * h_re)
                r, i = comp(spin, row, 0), comp(spin, row, 1)
                result[r] = re if column == 0 else result[r] + re
                result[i] = im if column == 0 else result[i] + im
    return result


def kernel(
    nlo,
    sp_hbm,
    g_hbm,
    out_ref,
    sp_ref,
    g_ref,
    stage,
    gstage,
    psi_in,
    g_in,
    links,
    field,
    tsend,
    trecv,
    ksend,
    krecv,
    klocal,
    ssend,
    srecv,
    ostage,
    o_in,
    send1,
    recv1,
    sendg,
    recvg,
    sendh,
    recvh,
    send2,
    recv2,
    local,
):
    nz = NHI * nlo
    nt = nz * NC
    f = lax.axis_index("fifth")
    p = lax.axis_index("space")
    y, zhi = lax.div(f, NHI), lax.rem(f, NHI)
    zlo, x, c = lax.div(p, NX * NC), lax.rem(lax.div(p, NC), NX), lax.rem(p, NC)
    z = zhi * nlo + zlo

    def device(dx, dy, dz, dc):
        return (dy * NHI + lax.div(dz, nlo), lax.rem(dz, nlo) * (NX * NC) + dx * NC + dc)

    def z_of(time):
        return lax.rem(Z_SIGN * lax.div(time, NC) + Z_OFFSET + nz, nz)

    z_to = z_of(p)
    upper = f >= 8
    folded = jnp.where(upper, 15 - f, f)
    y_to = lax.rem(NY - lax.div(folded, 2), NY)
    slot = jnp.where(upper, 2, 0) + lax.rem(folded, 2)
    flip = jnp.where(upper, 1, 0)
    ahead = lax.rem(z_to - zlo + nz, nz)
    gives_links = zhi == lax.rem(lax.div(ahead + nlo // 2, nlo), NHI)
    to_self = (y_to == y) & (z_to == z)
    t = lax.rem(Z_SIGN * (z - Z_OFFSET) + nz + nz, nz) * NC + c
    seg = lax.rem(NY - y, NY)
    sources = (2 * seg, 2 * seg + 1, 15 - 2 * seg, 14 - 2 * seg)
    ahead_me = lax.rem(z - lax.div(t, NX * NC) + nz, nz)
    link_hi = lax.rem(lax.div(ahead_me + nlo // 2, nlo), NHI)

    t_up, t_down = lax.rem(t + 1, nt), lax.rem(t + nt - 1, nt)
    near = {
        TP: device(x, y, z_of(t_up), lax.rem(t_up, NC)),
        TM: device(x, y, z_of(t_down), lax.rem(t_down, NC)),
        KP: device(lax.rem(x + 1, NX), y, z, c),
        KM: device(lax.rem(x + NX - 1, NX), y, z, c),
        SP: device(x, lax.rem(y + NY - 1, NY), z, c),
        SM: device(x, lax.rem(y + 1, NY), z, c),
    }

    barrier = pltpu.get_barrier_semaphore()

    def greet(device_id):
        pl.semaphore_signal(barrier, inc=1, device_id=device_id, device_id_type=MESH)

    for n in range(4):

        @pl.when(jnp.logical_not(to_self & (slot == n)))
        def _():
            greet((sources[n], t))

    for side in (TP, TM, KP, KM):
        greet(near[side])

    @pl.when(seg < NY - 1)
    def _():
        greet(near[SP])

    @pl.when(seg > 0)
    def _():
        greet(near[SM])

    for source, target, sem in ((sp_hbm, sp_ref, 2), (g_hbm, g_ref, 3)):
        pltpu.make_async_copy(source, target, local.at[sem]).start()
    pltpu.make_async_copy(sp_hbm, sp_ref, local.at[2]).wait()
    pltpu.make_async_copy(g_hbm, g_ref, local.at[3]).wait()

    for q in range(NX):
        for s in range(2):
            for b in range(3):
                row = pl.multiple_of(q * 48 + lax.rem(s + flip, 2) * 24 + b * 8, 8)
                stage[pl.ds(row, 8), :] = sp_ref[pl.ds((s * 24 + b * 8) * 4 + q, 8, stride=4), :]
        for mu in range(4):
            first = g_ref[pl.ds(mu * 72 + q, 8, stride=4), :]
            gstage[q * 48 + mu * 12 : q * 48 + mu * 12 + 8, :] = first
            last = g_ref[pl.ds(mu * 72 + 32 + q, 4, stride=4), :]
            gstage[q * 48 + mu * 12 + 8 : q * 48 + mu * 12 + 12, :] = last

    count = 8 - jnp.where(to_self, 1, 0) + jnp.where(seg > 0, 1, 0) + jnp.where(seg < NY - 1, 1, 0)
    pl.semaphore_wait(barrier, count)

    def block(ref, n):
        start = n * 48
        return ref.at[pl.ds(start if isinstance(n, int) else pl.multiple_of(start, 8), 48), :]

    def out_copy(q):
        return pltpu.make_async_remote_copy(
            src_ref=block(stage, q),
            dst_ref=block(psi_in, slot),
            send_sem=send1.at[q],
            recv_sem=recv1.at[slot],
            device_id=device(q, y_to, z_to, c),
            device_id_type=MESH,
        )

    def link_copy(q):
        return pltpu.make_async_remote_copy(
            src_ref=block(gstage, q),
            dst_ref=g_in,
            send_sem=sendg.at[q],
            recv_sem=recvg.at[0],
            device_id=device(q, y_to, z_to, c),
            device_id_type=MESH,
        )

    for q in range(NX):
        other = jnp.logical_not(to_self & (x == q))

        @pl.when(other & gives_links)
        def _():
            link_copy(q).start()

    for q in range(NX):

        @pl.when(jnp.logical_not(to_self & (x == q)))
        def _():
            out_copy(q).start()

    @pl.when(to_self)
    def _():
        mine = pltpu.make_async_copy(block(stage, x), block(psi_in, slot), local.at[0])
        mine.start()
        mine.wait()

    @pl.when(to_self & gives_links)
    def _():
        mine = pltpu.make_async_copy(block(gstage, x), g_in, local.at[1])
        mine.start()
        mine.wait()

    for n in range(24):
        field[0, n] = jnp.zeros((8, 128), jnp.float32)

    @pl.when(jnp.logical_not(to_self & (zhi == link_hi)))
    def _():
        link_copy(0).wait_recv()

    for mu in range(4):
        scale = -0.5 / filter_radius
        if mu == 3:
            scale = scale * jnp.where(t == nt - 1, -1.0, 1.0)
        rows = [
            jnp.broadcast_to(g_in[mu * 12 + r : mu * 12 + r + 1, :], (8, 128)) for r in range(12)
        ]
        for r in range(12):
            links[mu * 18 + r] = rows[r] * scale
        for i in range(3):
            j, k = (i + 1) % 3, (i + 2) % 3
            a_re, a_im, b_re, b_im = rows[2 * j], rows[2 * j + 1], rows[6 + 2 * k], rows[7 + 2 * k]
            c_re, c_im, d_re, d_im = rows[2 * k], rows[2 * k + 1], rows[6 + 2 * j], rows[7 + 2 * j]
            re = (a_re * b_re - a_im * b_im) - (c_re * d_re - c_im * d_im)
            im = (c_re * d_im + c_im * d_re) - (a_re * b_im + a_im * b_re)
            links[mu * 18 + 12 + 2 * i] = re * scale
            links[mu * 18 + 13 + 2 * i] = im * scale

    for n in range(4):

        @pl.when(jnp.logical_not(to_self & (slot == n)))
        def _():
            pltpu.make_async_remote_copy(
                src_ref=block(stage, 0),
                dst_ref=block(psi_in, n),
                send_sem=send1.at[0],
                recv_sem=recv1.at[n],
                device_id=near[TP],
                device_id_type=MESH,
            ).wait_recv()

    for n in range(24):
        field[1, n] = psi_in[pl.ds(n, 8, stride=24), :]

    lane = lax.broadcasted_iota(jnp.int32, (8, 128), 1)
    sub = lax.broadcasted_iota(jnp.int32, (8, 128), 0)
    low = lane < 64

    def shift(value, direction, forward):
        stride = 8**direction
        position = lax.rem(lax.div(lane, stride), 8)
        inside, outside = (128 - stride, 7 * stride) if forward else (stride, 128 - 7 * stride)
        edge = position == (7 if forward else 0)
        return jnp.where(edge, pltpu.roll(value, outside, 1), pltpu.roll(value, inside, 1))

    def half_turn(value):
        return pltpu.roll(value, 64, 1)

    def step(it, carry):
        def v(n):
            return field[it + 1, n]

        def link(mu):
            return lambda row, column, part: links[mu * 18 + (row * 3 + column) * 2 + part]

        def halo(side, source, target):
            return pltpu.make_async_remote_copy(
                src_ref=source,
                dst_ref=target,
                send_sem=sendh.at[it, side],
                recv_sem=recvh.at[it, side],
                device_id=near[side],
                device_id_type=MESH,
            )

        to_t_up = halo(TP, tsend.at[it, 0], trecv.at[it, 0])
        to_t_down = halo(TM, tsend.at[it, 1], trecv.at[it, 1])
        to_k_up = halo(KP, ksend.at[it, 0], krecv.at[it, 0])
        to_k_down = halo(KM, ksend.at[it, 1], krecv.at[it, 1])
        to_s_up = halo(SP, ssend.at[it, 0], srecv.at[it, 0])
        to_s_down = halo(SM, ssend.at[it, 1], srecv.at[it, 1])

        behind = colour_mul(link(3), project(v, 3, 1.0), True)
        for n in range(12):
            tsend[it, 0, n] = behind[n]
        to_t_up.start()
        front = project(v, 3, -1.0)
        for n in range(12):
            tsend[it, 1, n] = front[n]
        to_t_down.start()

        behind = colour_mul(link(2), project(v, 2, 1.0), True)
        for m in range(6):
            a, b = behind[2 * m], behind[2 * m + 1]
            ra, rb = half_turn(a), half_turn(b)
            ksend[it, 0, m] = jnp.where(low, ra, b)
            klocal[0, 2 * m] = ra
            klocal[0, 2 * m + 1] = rb
        to_k_up.start()
        front = project(v, 2, -1.0)
        for m in range(6):
            a, b = front[2 * m], front[2 * m + 1]
            ra, rb = half_turn(a), half_turn(b)
            ksend[it, 1, m] = jnp.where(low, a, rb)
            klocal[1, 2 * m] = ra
            klocal[1, 2 * m + 1] = rb
        to_k_down.start()

        for n in range(24):
            value = v(n)
            up, down = (3, 4) if n < 12 else (7, 0)
            ssend[it, 0, n : n + 1] = value[up : up + 1]
            ssend[it, 1, n : n + 1] = value[down : down + 1]

        @pl.when(seg < NY - 1)
        def _():
            to_s_up.start()

        @pl.when(seg > 0)
        def _():
            to_s_down.start()

        @pl.when(seg == NY - 1)
        def _():
            srecv[it, 1] = ssend[it, 0]

        @pl.when(seg == 0)
        def _():
            srecv[it, 0] = ssend[it, 1] * -quark_mass

        total = [((5.0 - wall_height) / filter_radius) * v(n) for n in range(24)]
        for direction in range(2):
            front = [shift(value, direction, True) for value in project(v, direction, -1.0)]
            add_rebuilt(total, colour_mul(link(direction), front, False), direction, -1.0)
            behind = colour_mul(link(direction), project(v, direction, 1.0), True)
            add_rebuilt(total, [shift(value, direction, False) for value in behind], direction, 1.0)

        to_k_up.wait_recv()
        behind = []
        for m in range(6):
            packed = krecv[it, 0, m]
            behind.append(jnp.where(low, packed, klocal[0, 2 * m]))
            behind.append(jnp.where(low, half_turn(packed), klocal[0, 2 * m + 1]))
        add_rebuilt(total, behind, 2, 1.0)
        to_k_down.wait_recv()
        front = []
        for m in range(6):
            packed = krecv[it, 1, m]
            front.append(jnp.where(low, klocal[1, 2 * m], half_turn(packed)))
            front.append(jnp.where(low, klocal[1, 2 * m + 1], packed))
        add_rebuilt(total, colour_mul(link(2), front, False), 2, -1.0)

        @pl.when(seg > 0)
        def _():
            to_s_up.wait_recv()

        @pl.when(seg < NY - 1)
        def _():
            to_s_down.wait_recv()

        for n in range(24):
            value = v(n)
            back, on = pltpu.roll(value, 1, 0), pltpu.roll(value, 7, 0)
            from_low = jnp.broadcast_to(srecv[it, 0, n : n + 1], (8, 128))
            from_high = jnp.broadcast_to(srecv[it, 1, n : n + 1], (8, 128))
            if n < 12:
                inner = jnp.where(sub < 4, back, on)
                moved = jnp.where(sub == 0, from_low, jnp.where(sub == 7, from_high, inner))
            else:
                inner = jnp.where(sub < 4, on, back)
                moved = jnp.where(sub == 4, from_low, jnp.where(sub == 3, from_high, inner))
            total[n] = total[n] - (1.0 / filter_radius) * moved

        to_t_up.wait_recv()
        add_rebuilt(total, [trecv[it, 0, n] for n in range(12)], 3, 1.0)
        to_t_down.wait_recv()
        front = [trecv[it, 1, n] for n in range(12)]
        add_rebuilt(total, colour_mul(link(3), front, False), 3, -1.0)

        gain = jnp.where(it == 0, 1.0, 2.0)
        for n in range(24):
            signed = pltpu.roll(total[n], 4, 0)
            centred = (filter_center / filter_radius) * v(n)
            inner = (signed if n < 12 else -signed) - centred
            field[it + 2, n] = gain * inner - field[it, n]
        return carry

    lax.fori_loop(0, DEGREE, step, 0)

    for n in range(24):
        ostage[pl.ds(n, 8, stride=24), :] = field[DEGREE + 1, n]

    def back_copy(n):
        return pltpu.make_async_remote_copy(
            src_ref=block(ostage, n),
            dst_ref=block(o_in, x),
            send_sem=send2.at[n],
            recv_sem=recv2.at[x],
            device_id=(sources[n], t),
            device_id_type=MESH,
        )

    for hi in range(NHI):
        for n in range(4):

            @pl.when(jnp.logical_not(to_self & (slot == n)) & (lax.rem(sources[n], NHI) == hi))
            def _():
                back_copy(n).start()

        if hi < NHI - 1:
            for n in range(4):

                @pl.when(jnp.logical_not(to_self & (slot == n)) & (lax.rem(sources[n], NHI) == hi))
                def _():
                    back_copy(n).wait_send()

    @pl.when(to_self)
    def _():
        mine = pltpu.make_async_copy(block(ostage, slot), block(o_in, x), local.at[0])
        mine.start()
        mine.wait()

    for q in range(NX):

        @pl.when(jnp.logical_not(to_self & (x == q)))
        def _():
            pltpu.make_async_remote_copy(
                src_ref=block(ostage, 0),
                dst_ref=block(o_in, q),
                send_sem=send2.at[0],
                recv_sem=recv2.at[q],
                device_id=near[TP],
                device_id_type=MESH,
            ).wait_recv()

        for s in range(2):
            for b in range(3):
                row = pl.multiple_of(q * 48 + lax.rem(s + flip, 2) * 24 + b * 8, 8)
                out_ref[pl.ds((s * 24 + b * 8) * 4 + q, 8, stride=4), :] = o_in[pl.ds(row, 8), :]

    for q in range(NX):
        other = jnp.logical_not(to_self & (x == q))

        @pl.when(other)
        def _():
            out_copy(q).wait_send()

        @pl.when(other & gives_links)
        def _():
            link_copy(q).wait_send()

    def sent(it, carry):
        def left(side, source, target):
            pltpu.make_async_remote_copy(
                src_ref=source,
                dst_ref=target,
                send_sem=sendh.at[it, side],
                recv_sem=recvh.at[it, side],
                device_id=near[side],
                device_id_type=MESH,
            ).wait_send()

        left(TP, tsend.at[it, 0], trecv.at[it, 0])
        left(TM, tsend.at[it, 1], trecv.at[it, 1])
        left(KP, ksend.at[it, 0], krecv.at[it, 0])
        left(KM, ksend.at[it, 1], krecv.at[it, 1])

        @pl.when(seg < NY - 1)
        def _():
            left(SP, ssend.at[it, 0], srecv.at[it, 0])

        @pl.when(seg > 0)
        def _():
            left(SM, ssend.at[it, 1], srecv.at[it, 1])

        return carry

    lax.fori_loop(0, DEGREE, sent, 0)

    for n in range(4):

        @pl.when(jnp.logical_not(to_self & (slot == n)) & (lax.rem(sources[n], NHI) == NHI - 1))
        def _():
            back_copy(n).wait_send()


def solution(mesh):
    nlo = mesh.shape["space"] // (NX * NC)
    vmem = pl.BlockSpec(memory_space=pltpu.VMEM)

    def f32(*shape):
        return pltpu.VMEM(shape, jnp.float32)

    dma = pltpu.SemaphoreType.DMA

    def on_device(spinor, gauge_links):
        out = pl.pallas_call(
            functools.partial(kernel, nlo),
            out_shape=jax.ShapeDtypeStruct((192, 128), jnp.float32),
            in_specs=[pl.BlockSpec(memory_space=pltpu.HBM)] * 2,
            out_specs=vmem,
            scratch_shapes=[
                f32(192, 128),
                f32(288, 128),
                f32(192, 128),
                f32(192, 128),
                f32(192, 128),
                f32(48, 128),
                f32(72, 8, 128),
                f32(DEGREE + 2, 24, 8, 128),
                f32(DEGREE, 2, 12, 8, 128),
                f32(DEGREE, 2, 12, 8, 128),
                f32(DEGREE, 2, 6, 8, 128),
                f32(DEGREE, 2, 6, 8, 128),
                f32(2, 12, 8, 128),
                f32(DEGREE, 2, 24, 128),
                f32(DEGREE, 2, 24, 128),
                f32(192, 128),
                f32(192, 128),
                dma((4,)),
                dma((4,)),
                dma((4,)),
                dma((1,)),
                dma((DEGREE, 6)),
                dma((DEGREE, 6)),
                dma((4,)),
                dma((4,)),
                dma((4,)),
            ],
            compiler_params=pltpu.CompilerParams(
                collective_id=0, has_side_effects=True, vmem_limit_bytes=55104 * 1024
            ),
        )(spinor.reshape(192, 128), gauge_links.reshape(288, 128))
        return out.reshape(2, 24, 1, 512)

    return jax.shard_map(
        on_device,
        mesh=mesh,
        in_specs=(P("fifth", None, "space", None), P(None, None, "space", None)),
        out_specs=P("fifth", None, "space", None),
        check_vma=False,
    )
```
